256 devices in a mesh: dp: 32 (over x, y, core), expert: 8 (over z).
Axes of the slice: x: 4, y: 4, z: 8, core: 2. Of those that a mesh axis runs over, the one named last changes fastest.
Arguments:
- tokens: bfloat16 [32768, 4096], P(('dp', 'expert')), may hold values from -6 to 6
- router_weight: float32 [4096, 128], replicated, may hold values from -0.1875 to 0.1875
- rollout_ids: int32 [32768, 8], P(('dp', 'expert')), may hold values from 0 to 127, all different within a row; in each aligned block of 128 rows (0 to 127, 128 to 255, ...) at most 9 rows name the same one
- source_row: int32 [32768], P(('dp', 'expert')), may hold values from 0 to 32767, as said below
- gate_weight: bfloat16 [32, 4096, 1536], P('dp', None, 'expert'), may hold values from -0.09375 to 0.09375
- up_weight: bfloat16 [32, 4096, 1536], P('dp', None, 'expert'), may hold values from -0.09375 to 0.09375
- down_weight: bfloat16 [32, 1536, 4096], P('dp', None, 'expert'), may hold values from -0.15625 to 0.15625
Outputs:
- layer_out: bfloat16 [32768, 4096], P(('dp', 'expert'))
The draws below stay inside these ranges and needn't reach their ends.
Inputs may be any that keep to these rules, and one draw needn't show every extreme that they name: `rollout_ids`: each row names 8 different experts. In every aligned block of 128 rows no expert is named by more than 9 rows, a bound that some block reaches. `source_row`: A permutation of the 32768 rows. The 128 trainer rows of an aligned block all read rows of one aligned block of 128 rollout rows, the blocks correspond one to one, and a trainer block's index and its rollout block's index are equal modulo 8.
All inputs are finite; a program needn't handle non-finite values.
Results may differ from the reference program's by a relative error of at most 0.0058.
Values may be sent and summed in bfloat16 or wider, within the bound.
No kernel may reach another device: no remote copies, remote signals or barrier semaphores. Data moves between devices by JAX's collectives and lax.ppermute only.
A program may use at most 128 MiB of HBM per device.

```python
import math
import jax
import jax.numpy as jnp
import numpy as np
from jax import lax

D = 4096
FF = 1536
EXPERTS = 128
TOP = 8
TOK_DEV = 128
CAP = 9
WINDOW = 32
COLUMNS = 8
TOKENS = 32768


def draw_source_row(key, part):
    key = jax.random.fold_in(key, 7)
    key_blocks, key_rows = jax.random.split(key)
    block_keys = jax.random.split(key_blocks, COLUMNS)
    chosen = jax.vmap(lambda single: jax.random.permutation(single, WINDOW))(block_keys)
    row_keys = jax.random.split(key_rows, WINDOW * COLUMNS)
    inner = jax.vmap(lambda single: jax.random.permutation(single, TOK_DEV))(row_keys)
    inner = inner.reshape(WINDOW, COLUMNS, TOK_DEV).astype(jnp.int32)
    source_dp = jnp.transpose(chosen).astype(jnp.int32)[:, :, None]
    column = jnp.arange(COLUMNS, dtype=jnp.int32)[None, :, None]
    rows_out = (source_dp * COLUMNS + column) * TOK_DEV + inner
    return rows_out.reshape(TOKENS).astype(jnp.int32)


def steps_of(own_key, dims, cuts, smallest, largest):
    gain, own = 1.0, jax.random.fold_in(own_key, 6)
    for axis_at, blocks in cuts:
        draws = jnp.exp(jax.random.uniform(jax.random.fold_in(own, axis_at), (blocks,), jnp.float32, smallest / len(cuts), largest / len(cuts)))
        gain = gain * jnp.repeat(draws, dims[axis_at] // blocks).reshape([-1 if axis == axis_at else 1 for axis in range(len(dims))])
    return gain


def routed_block(key, own, number, rows, amount, top, most, skew):
    ranking = jax.random.permutation(key, amount)
    heavy_load, common = load_shares(amount, rows * top, most, skew, True), load_shares(amount, rows * top, most, skew, False)
    places = jnp.arange(amount)

    def named(sizes, offset_by):
        used = int((sizes > 0).sum())
        fixed = max(1, used // 4)
        passed = fixed + (places - fixed + offset_by * (used - fixed)) % max(1, amount - fixed)
        return jnp.zeros((amount,), jnp.int32).at[ranking[jnp.where(places < fixed, places, passed)]].set(jnp.asarray(sizes, jnp.int32))

    sizes = jnp.where(number % 4 == 0, named(heavy_load, number // 4), named(common, number - number // 4 - 1))
    mixed = jax.random.permutation(jax.random.fold_in(own, 3), amount)
    giver, receiver = mixed[0:amount // 2 * 2:2], mixed[1:amount // 2 * 2:2]
    room = jnp.minimum(sizes[giver] - 1, most - sizes[receiver]) // 2
    room = jnp.where((giver == ranking[0]) | (receiver == ranking[0]) | (sizes[receiver] == 0), 0, jnp.maximum(room, 0))
    passed = jax.random.randint(jax.random.fold_in(own, 4), (amount // 2,), 0, 1 << 20) % (room + 1)
    sizes = sizes.at[giver].add(-passed).at[receiver].add(passed)
    items = jnp.searchsorted(jnp.cumsum(sizes), jnp.arange(rows * top), side="right").astype(jnp.int32)
    listing = items.reshape(top, rows).T
    listing = listing[jax.random.permutation(jax.random.fold_in(own, 1), rows)]
    offset_by = jax.random.randint(jax.random.fold_in(own, 2), (rows, 1), 0, top)
    return jnp.take_along_axis(listing, (jnp.arange(top)[None, :] + offset_by) % top, axis=1)


def load_shares(amount, total, reach, slope, full):
    loads = [(1 << 20) // math.isqrt(standing ** slope) + 1 for standing in range(1, amount + 1)]
    largest = reach if full else min(reach, max(-(-total // amount), total * loads[0] // sum(loads)))
    least = 1 if total - largest >= amount - 1 else 0
    counts, surplus = [largest] + [least] * (amount - 1), total - largest - least * (amount - 1)
    while surplus > 0:
        candidates = [i for i in range(1, amount) if counts[i] < largest] or [i for i in range(1, amount) if counts[i] < reach]
        mass, left = sum([loads[i] for i in candidates]), surplus
        for i in candidates:
            extra = min(reach - counts[i], max(1, left * loads[i] // mass), surplus)
            counts[i] = counts[i] + extra
            surplus = surplus - extra
    return np.array(counts)


def centred(stream_key, extent, width, bound, cuts=(), held_as=jnp.bfloat16):
    entries = jax.random.normal(stream_key, extent, jnp.float32) * width
    if len(cuts) > 0:
        entries = steps_of(stream_key, extent, cuts, -0.22, 0.18) * entries
    return jnp.clip(entries, min=-bound, max=bound).astype(held_as)


def setup_inputs(seed: int = 0) -> dict:
    key_of = jax.random.split(jax.random.key(seed), 8)
    tokens = centred(key_of[0], (TOKENS, D), 1.0, 6.0, ((0, 256),))
    router_weight = centred(key_of[1], (D, EXPERTS), (D // 4) ** -0.5, 0.1875, (), jnp.float32)
    rollout_ids_keys = jax.random.split(jax.random.fold_in(key_of[2], 1), TOKENS // TOK_DEV)
    rollout_ids_turns = jax.random.permutation(jax.random.fold_in(key_of[2], 3), TOKENS // TOK_DEV)
    rollout_ids = jax.vmap(lambda own, number: routed_block(jax.random.fold_in(key_of[2], 2), own, number, TOK_DEV, EXPERTS, TOP, CAP, 1))(rollout_ids_keys, rollout_ids_turns).reshape((TOKENS, TOP))
    source_row = draw_source_row(jax.random.fold_in(key_of[7], 71), 0)
    gate_weight = centred(key_of[4], (WINDOW, D, FF), D ** -0.5, 0.09375, ((0, 32), (2, 8)))
    up_weight = centred(key_of[5], (WINDOW, D, FF), D ** -0.5, 0.09375, ((0, 32), (2, 8)))
    down_weight = centred(key_of[6], (WINDOW, FF, D), FF ** -0.5, 0.15625, ((0, 32), (2, 8)))
    return {"tokens": tokens, "router_weight": router_weight, "rollout_ids": rollout_ids, "source_row": source_row, "gate_weight": gate_weight, "up_weight": up_weight, "down_weight": down_weight}


def reference(tokens, router_weight, rollout_ids, source_row, gate_weight, up_weight, down_weight):
    expert_ids = jnp.take(rollout_ids, source_row, axis=0)
    logits = jnp.dot(tokens.astype(jnp.float32), router_weight, precision=lax.Precision.HIGHEST)
    picked = jnp.take_along_axis(logits, expert_ids, axis=1)
    raised = jnp.exp(picked)
    weights = raised / jnp.sum(raised, axis=1, keepdims=True)
    row_limit = TOKENS // TOK_DEV * CAP

    def one_expert(combined, inputs):
        gate_mat, up_mat, down_mat, expert_index = inputs
        matches = expert_ids == expert_index
        used = jnp.any(matches, axis=1)
        pick_share = jnp.sum(jnp.where(matches, weights, 0.0), axis=1)
        row_index = jnp.nonzero(used, size=row_limit, fill_value=0)[0].astype(jnp.int32)
        rows_in = jnp.take(tokens, row_index, axis=0)
        gate_val = jnp.dot(rows_in, gate_mat, preferred_element_type=jnp.float32)
        upward = jnp.dot(rows_in, up_mat, preferred_element_type=jnp.float32)
        hidden = (jax.nn.silu(gate_val) * upward).astype(jnp.bfloat16)
        result = jnp.dot(hidden, down_mat, preferred_element_type=jnp.float32).astype(jnp.bfloat16)
        live = jnp.arange(row_limit) < jnp.sum(used.astype(jnp.int32))
        factor = jnp.where(live, jnp.take(pick_share, row_index), 0.0)
        combined = combined.at[row_index].add(factor[:, None] * result.astype(jnp.float32))
        return combined, None

    combined = jnp.zeros((TOKENS, D), jnp.float32)
    combined, unused = lax.scan(one_expert, combined, (gate_weight, up_weight, down_weight, jnp.arange(WINDOW, dtype=jnp.int32)))
    return combined.astype(jnp.bfloat16)
```

```python
import jax
import jax.numpy as jnp
from jax import lax
from jax.sharding import PartitionSpec as P

MAIN = 8


def per_device(tokens, router_weight, rollout_ids, source_row, gate_weight, up_weight, down_weight):
    owners = lax.axis_size("dp")
    columns = lax.axis_size("expert")
    tok_rows, model_width = tokens.shape
    top_count = rollout_ids.shape[1]
    out_width = down_weight.shape[2]
    bf16, f32 = jnp.bfloat16, jnp.float32

    sent_ids = jnp.broadcast_to(rollout_ids.T[None], (owners, top_count, tok_rows))
    blocks = lax.all_to_all(sent_ids, "dp", split_axis=0, concat_axis=0, tiled=True)
    source_block = source_row[0] // (tok_rows * columns)
    block = lax.dynamic_index_in_dim(blocks, source_block, axis=0, keepdims=False)
    place = (source_row % tok_rows)[None, :] == jnp.arange(tok_rows, dtype=jnp.int32)[:, None]
    expert_ids = jnp.dot(
        block.astype(bf16), place.astype(bf16), preferred_element_type=f32
    ).astype(jnp.int32).T

    logits = jnp.dot(tokens.astype(f32), router_weight, precision=lax.Precision.HIGHEST)
    expert_iota = jnp.arange(router_weight.shape[1], dtype=jnp.int32)
    picks = jnp.any(expert_ids[:, :, None] == expert_iota[None, None, :], axis=1)
    raised = jnp.where(picks, jnp.exp(jnp.where(picks, logits, 0.0)), 0.0)
    weights = raised / jnp.sum(raised, axis=1, keepdims=True)
    pick_weight = weights[:, :owners]
    chosen = picks[:, :owners]
    before = jnp.arange(tok_rows)[:, None] > jnp.arange(tok_rows)[None, :]
    slot_rank = jnp.dot(before.astype(bf16), chosen.astype(bf16), preferred_element_type=f32)
    slot_rank = jnp.where(chosen, slot_rank, -1.0)

    def selector(rank, first, count):
        slots = jnp.arange(first, first + count, dtype=f32)
        return rank[..., :, :, None] == slots

    sel_main = selector(slot_rank, 0, MAIN).reshape(tok_rows, owners * MAIN).astype(bf16)
    sel_last = selector(slot_rank, MAIN, 1).reshape(tok_rows, owners).astype(bf16)

    def dispatch(sel, rows):
        out = lax.dot_general(sel, tokens, (((0,), (0,)), ((), ())), preferred_element_type=f32)
        out = out.astype(bf16).reshape(owners, rows, model_width)
        out = lax.all_to_all(out, "dp", split_axis=0, concat_axis=0, tiled=True)
        return out.reshape(owners * rows, model_width)

    arrived_main = dispatch(sel_main, MAIN)
    arrived_last = dispatch(sel_last, 1)

    info = jnp.concatenate([pick_weight, slot_rank], axis=1)
    infos = lax.all_gather(info, "expert", axis=0)

    gate_part = gate_weight[0]
    up_part = up_weight[0]
    down_part = down_weight[0]

    def expert(arrived):
        rows = lax.all_gather(arrived, "expert", axis=0, tiled=True)
        gate_val = lax.dot_general(gate_part, rows, (((0,), (1,)), ((), ())), preferred_element_type=f32)
        upward = lax.dot_general(up_part, rows, (((0,), (1,)), ((), ())), preferred_element_type=f32)
        hidden = (jax.nn.silu(gate_val) * upward).astype(bf16)
        full = lax.all_gather(hidden, "expert", axis=0, tiled=True)
        return lax.dot_general(
            full, down_part, (((0,), (0,)), ((), ())), preferred_element_type=f32
        ).astype(bf16)

    out_main = expert(arrived_main).reshape(columns, owners, MAIN, out_width)
    out_last = expert(arrived_last).reshape(columns, owners, 1, out_width)

    def give_back(out):
        return lax.all_to_all(out, "dp", split_axis=1, concat_axis=1, tiled=True)

    back_main = give_back(out_main).reshape(columns, owners * MAIN, out_width)
    back_last = give_back(out_last).reshape(columns, owners, out_width)

    weight_all = infos[:, :, :owners]
    rank_all = infos[:, :, owners:]

    def combine(first, count, back):
        mat = jnp.where(selector(rank_all, first, count), weight_all[..., None], 0.0)
        mat = mat.reshape(columns, tok_rows, owners * count)
        high = mat.astype(bf16)
        low = (mat - high.astype(f32)).astype(bf16)
        dims = (((2,), (1,)), ((0,), (0,)))
        return lax.dot_general(high, back, dims, preferred_element_type=f32) + lax.dot_general(
            low, back, dims, preferred_element_type=f32
        )

    part = (combine(0, MAIN, back_main) + combine(MAIN, 1, back_last)).astype(bf16)
    whole = lax.all_to_all(part, "expert", split_axis=0, concat_axis=0, tiled=True)
    return jnp.transpose(whole, (1, 0, 2)).reshape(tok_rows, model_width)


def solution(mesh):
    in_specs = (
        P(("dp", "expert"), None),
        P(),
        P(("dp", "expert"), None),
        P(("dp", "expert")),
        P("dp", None, "expert"),
        P("dp", None, "expert"),
        P("dp", None, "expert"),
    )
    out_specs = P(("dp", "expert"), None)
    return jax.shard_map(
        per_device, mesh=mesh, in_specs=in_specs, out_specs=out_specs, check_vma=False
    )
```

```python
import jax
import jax.numpy as jnp
from jax import lax
from jax.sharding import PartitionSpec as P

MAIN = 8
FIRST_WIDTH = 1664


def per_device(tokens, router_weight, rollout_ids, source_row, gate_weight, up_weight, down_weight):
    owners = lax.axis_size("dp")
    columns = lax.axis_size("expert")
    tok_rows, model_width = tokens.shape
    top_count = rollout_ids.shape[1]
    hidden_part = gate_weight.shape[2]
    out_width = down_weight.shape[2]
    bf16, f32 = jnp.bfloat16, jnp.float32
    block_rows = columns * (MAIN + 1)
    slot_rows = owners * block_rows
    row_toks = columns * tok_rows
    first = FIRST_WIDTH
    second = model_width - first
    fold = -(-second // (MAIN * 128)) * 128

    raw = lax.all_gather(tokens[:, :first], "expert", axis=0, tiled=True)

    logits = jnp.dot(tokens.astype(f32), router_weight, precision=lax.Precision.HIGHEST)

    sent_ids = jnp.broadcast_to(rollout_ids.T[None], (owners, top_count, tok_rows))
    blocks = lax.all_to_all(sent_ids, "dp", split_axis=0, concat_axis=0, tiled=True)
    source_block = source_row[0] // (tok_rows * columns)
    block = lax.dynamic_index_in_dim(blocks, source_block, axis=0, keepdims=False)
    place = (source_row % tok_rows)[None, :] == jnp.arange(tok_rows, dtype=jnp.int32)[:, None]
    expert_ids = jnp.dot(
        block.astype(bf16), place.astype(bf16), preferred_element_type=f32
    ).astype(jnp.int32).T

    expert_iota = jnp.arange(router_weight.shape[1], dtype=jnp.int32)
    picks = jnp.any(expert_ids[:, :, None] == expert_iota[None, None, :], axis=1)
    chosen = picks[:, :owners]
    before = jnp.arange(tok_rows)[:, None] > jnp.arange(tok_rows)[None, :]
    slot_rank = jnp.dot(before.astype(bf16), chosen.astype(bf16), preferred_element_type=f32)
    slot_rank = jnp.where(chosen, slot_rank, -1.0)

    def select(lowest, count):
        slots = jnp.arange(lowest, lowest + count, dtype=f32)
        sel = slot_rank[:, :, None] == slots
        sel = sel.reshape(tok_rows, owners * count).astype(bf16)
        return lax.dot_general(
            sel, tokens[:, first:], (((0,), (0,)), ((), ())), preferred_element_type=f32
        ).astype(bf16)

    sent_main = select(0, MAIN).reshape(owners, MAIN, second)
    sent_last = jnp.pad(select(MAIN, 1), ((0, 0), (0, MAIN * fold - second)))
    sent_last = sent_last.reshape(owners, MAIN, fold)
    sent = jnp.concatenate([sent_main, sent_last], axis=2)
    arrived = lax.all_to_all(sent, "dp", split_axis=0, concat_axis=0, tiled=True)
    gathered = lax.all_gather(
        arrived.reshape(owners * MAIN, second + fold), "expert", axis=0, tiled=True
    )

    raised = jnp.where(picks, jnp.exp(jnp.where(picks, logits, 0.0)), 0.0)
    weights = raised / jnp.sum(raised, axis=1, keepdims=True)
    info = jnp.concatenate([slot_rank, weights[:, :owners]], axis=1).T
    infos = lax.all_to_all(
        jnp.broadcast_to(info[None], (columns,) + info.shape), "expert", 0, 0, tiled=True
    )
    infos = jnp.transpose(infos, (1, 0, 2)).reshape(2 * owners, 1, row_toks)
    row_rank, row_weight = infos[:owners], infos[owners:]

    row = jnp.arange(block_rows, dtype=jnp.int32)
    is_main = row < columns * MAIN
    row_column = jnp.where(is_main, row // MAIN, row - columns * MAIN)
    row_slot = jnp.where(is_main, row % MAIN, MAIN).astype(f32)
    tok_column = jnp.arange(row_toks, dtype=jnp.int32) // tok_rows
    same_column = row_column[:, None] == tok_column[None, :]
    taken = (row_rank == row_slot[None, :, None]) & same_column[None]

    first_sent = jnp.dot(
        taken.reshape(slot_rows, row_toks).astype(bf16), raw, preferred_element_type=f32
    ).astype(bf16)
    first_rows = lax.all_to_all(
        first_sent.reshape(owners, block_rows, first), "dp", split_axis=0, concat_axis=0, tiled=True
    ).reshape(slot_rows, first)

    both = jnp.concatenate([gate_weight[0], up_weight[0]], axis=1)
    first_val = jnp.dot(first_rows, both[:first], preferred_element_type=f32)
    first_val = first_val.reshape(owners, block_rows, 2 * hidden_part)

    wide = jnp.pad(both[first:], ((0, fold), (0, 0)))
    main_val = jnp.dot(gathered, wide, preferred_element_type=f32)
    main_val = main_val.reshape(columns, owners, MAIN, 2 * hidden_part)
    main_val = jnp.transpose(main_val, (1, 0, 2, 3)).reshape(owners, columns * MAIN, 2 * hidden_part)
    last_rows = gathered[:, second:].reshape(columns * owners, MAIN * fold)[:, :second]
    last_val = jnp.dot(last_rows, both[first:], preferred_element_type=f32)
    last_val = jnp.transpose(last_val.reshape(columns, owners, 2 * hidden_part), (1, 0, 2))
    value = first_val + jnp.concatenate([main_val, last_val], axis=1)
    value = value.reshape(slot_rows, 2 * hidden_part)
    hidden = (jax.nn.silu(value[:, :hidden_part]) * value[:, hidden_part:]).astype(bf16)

    full = lax.all_gather(hidden, "expert", axis=1, tiled=True)
    out = jnp.dot(full, down_weight[0], preferred_element_type=f32).astype(bf16)
    back = lax.all_to_all(
        out.reshape(owners, block_rows, out_width), "dp", split_axis=0, concat_axis=0, tiled=True
    ).reshape(slot_rows, out_width)

    mat = jnp.where(taken, row_weight, 0.0).reshape(slot_rows, row_toks)
    high = lax.reduce_precision(mat, 8, 7)
    low = (mat - high).astype(bf16)
    dims = (((0,), (0,)), ((), ()))
    part = lax.dot_general(high.astype(bf16), back, dims, preferred_element_type=f32)
    part = part + lax.dot_general(low, back, dims, preferred_element_type=f32)
    part = part.astype(bf16).reshape(columns, tok_rows, out_width)
    whole = lax.all_to_all(part, "expert", split_axis=0, concat_axis=0, tiled=True)
    return jnp.transpose(whole, (1, 0, 2)).reshape(tok_rows, model_width)


def solution(mesh):
    in_specs = (
        P(("dp", "expert"), None),
        P(),
        P(("dp", "expert"), None),
        P(("dp", "expert")),
        P("dp", None, "expert"),
        P("dp", None, "expert"),
        P("dp", None, "expert"),
    )
    out_specs = P(("dp", "expert"), None)
    return jax.shard_map(
        per_device, mesh=mesh, in_specs=in_specs, out_specs=out_specs, check_vma=False
    )
```

```python
import functools

import jax
import jax.numpy as jnp
from jax import lax
from jax.experimental import pallas as pl
from jax.experimental.pallas import tpu as pltpu
from jax.sharding import PartitionSpec as P

MAIN = 8
FIRST_WIDTH = 1792
STEP = 256
VMEM_BYTES = 48 * 1024 * 1024
bf16, f32 = jnp.bfloat16, jnp.float32


def iota(shape, dim):
    return lax.broadcasted_iota(jnp.int32, shape, dim)


def first_dispatch_kernel(columns, tok_rows, rank_ref, raw_ref, out_ref, pair_sel, last_sel):
    owners = rank_ref.shape[0]
    pairs = columns // 2
    pair_toks, pair_rows = 2 * tok_rows, 2 * MAIN

    @pl.when(pl.program_id(0) == 0)
    def _():
        row, tok = iota((pair_rows, pair_toks), 0), iota((pair_rows, pair_toks), 1)
        wanted = jnp.where(row // MAIN == tok // tok_rows, row % MAIN, -2).astype(f32)
        for pair in range(pairs):
            rank = rank_ref[:, :, pair * pair_toks : (pair + 1) * pair_toks]
            sel = jnp.where(rank == wanted[None], 1.0, 0.0).astype(bf16)
            pair_sel[pair] = sel.reshape(owners * pair_rows, pair_toks)
        row, tok = iota((columns, columns * tok_rows), 0), iota((columns, columns * tok_rows), 1)
        wanted = jnp.where(row == tok // tok_rows, MAIN, -2).astype(f32)
        sel = jnp.where(rank_ref[...] == wanted[None], 1.0, 0.0)
        last_sel[...] = sel.reshape(owners * columns, columns * tok_rows).astype(bf16)

    for pair in range(pairs):
        rows = jnp.dot(
            pair_sel[pair],
            raw_ref[pair * pair_toks : (pair + 1) * pair_toks, :],
            preferred_element_type=f32,
        ).astype(bf16)
        out_ref[:, pair * pair_rows : (pair + 1) * pair_rows, :] = rows.reshape(
            owners, pair_rows, rows.shape[1]
        )
    rows = jnp.dot(last_sel[...], raw_ref[...], preferred_element_type=f32)
    out_ref[:, columns * MAIN :, :] = rows.reshape(owners, columns, rows.shape[1]).astype(bf16)


def first_dispatch(rank, raw, columns, tok_rows):
    owners = rank.shape[0]
    row_toks, width = raw.shape
    block_rows = columns * (MAIN + 1)
    pairs = columns // 2
    return pl.pallas_call(
        functools.partial(first_dispatch_kernel, columns, tok_rows),
        grid=(width // STEP,),
        in_specs=[
            pl.BlockSpec((owners, 1, row_toks), lambda f: (0, 0, 0)),
            pl.BlockSpec((row_toks, STEP), lambda f: (0, f)),
        ],
        out_specs=pl.BlockSpec((owners, block_rows, STEP), lambda f: (0, 0, f)),
        out_shape=jax.ShapeDtypeStruct((owners, block_rows, width), bf16),
        scratch_shapes=[
            pltpu.VMEM((pairs, owners * 2 * MAIN, 2 * tok_rows), bf16),
            pltpu.VMEM((owners * columns, row_toks), bf16),
        ],
        compiler_params=pltpu.CompilerParams(vmem_limit_bytes=VMEM_BYTES),
    )(rank, raw)


def hidden_kernel(main_steps, x_ref, w_ref, v_ref, o_ref):
    columns, rows, width = x_ref.shape
    half = w_ref.shape[1] // 2
    acc = jnp.dot(x_ref[...].reshape(columns * rows, width), w_ref[...], preferred_element_type=f32)

    def finish(acc):
        val = acc + v_ref[...]
        gate, up = val[:, :half], val[:, half:]
        hidden = gate / (1.0 + jnp.exp(-gate)) * up
        o_ref[...] = hidden.T[: o_ref.shape[0]].astype(bf16)

    @pl.when(pl.program_id(0) < main_steps)
    def _():
        pieces = [
            acc[(j * rows + i) : (j * rows + i + MAIN)]
            for i in range(0, rows, MAIN)
            for j in range(columns)
        ]
        finish(jnp.concatenate(pieces, axis=0))

    @pl.when(pl.program_id(0) == main_steps)
    def _():
        finish(acc)


def hidden_rows(gathered, weight, first_val, hidden_part):
    columns, col_rows, width = gathered.shape
    steps = MAIN + 1
    rows = col_rows // steps
    step_rows = columns * rows
    return pl.pallas_call(
        functools.partial(hidden_kernel, MAIN),
        grid=(steps,),
        in_specs=[
            pl.BlockSpec((columns, rows, width), lambda b: (0, b, 0)),
            pl.BlockSpec(weight.shape, lambda b: (0, 0)),
            pl.BlockSpec((step_rows, weight.shape[1]), lambda b: (b, 0)),
        ],
        out_specs=pl.BlockSpec((hidden_part, step_rows), lambda b: (0, b)),
        out_shape=jax.ShapeDtypeStruct((hidden_part, steps * step_rows), bf16),
        compiler_params=pltpu.CompilerParams(vmem_limit_bytes=VMEM_BYTES),
    )(gathered, weight, first_val)


def per_device(tokens, router_weight, rollout_ids, source_row, gate_weight, up_weight, down_weight):
    owners = lax.axis_size("dp")
    columns = lax.axis_size("expert")
    tok_rows, model_width = tokens.shape
    top_count = rollout_ids.shape[1]
    hidden_part = gate_weight.shape[2]
    out_width = down_weight.shape[2]
    block_rows = columns * (MAIN + 1)
    slot_rows = owners * block_rows
    row_toks = columns * tok_rows
    first = FIRST_WIDTH
    second = model_width - first
    fold = -(-second // (MAIN * 128)) * 128
    main_rows = owners * columns * MAIN

    raw = lax.all_gather(tokens[:, :first], "expert", axis=0, tiled=True)

    logits = jnp.dot(tokens.astype(f32), router_weight, precision=lax.Precision.HIGHEST)

    sent_ids = jnp.broadcast_to(rollout_ids.T[None], (owners, top_count, tok_rows))
    blocks = lax.all_to_all(sent_ids, "dp", split_axis=0, concat_axis=0, tiled=True)
    source_block = source_row[0] // (tok_rows * columns)
    block = lax.dynamic_index_in_dim(blocks, source_block, axis=0, keepdims=False)
    place = (source_row % tok_rows)[None, :] == jnp.arange(tok_rows, dtype=jnp.int32)[:, None]
    expert_ids = jnp.dot(
        block.astype(bf16), place.astype(bf16), preferred_element_type=f32
    ).astype(jnp.int32).T

    expert_iota = jnp.arange(router_weight.shape[1], dtype=jnp.int32)
    picks = jnp.any(expert_ids[:, :, None] == expert_iota[None, None, :], axis=1)
    chosen = picks[:, :owners]
    before = jnp.arange(tok_rows)[:, None] > jnp.arange(tok_rows)[None, :]
    slot_rank = jnp.dot(before.astype(bf16), chosen.astype(bf16), preferred_element_type=f32)
    slot_rank = jnp.where(chosen, slot_rank, -1.0)

    def whole_row(info):
        sent = jnp.broadcast_to(info.T[None], (columns, owners, tok_rows))
        got = lax.all_to_all(sent, "expert", split_axis=0, concat_axis=0, tiled=True)
        return jnp.transpose(got, (1, 0, 2)).reshape(owners, 1, row_toks)

    row_rank = whole_row(slot_rank.astype(bf16)).astype(f32)

    def select(lowest, count):
        slots = jnp.arange(lowest, lowest + count, dtype=f32)
        sel = slot_rank[:, :, None] == slots
        sel = sel.reshape(tok_rows, owners * count).astype(bf16)
        return lax.dot_general(
            sel, tokens[:, first:], (((0,), (0,)), ((), ())), preferred_element_type=f32
        ).astype(bf16)

    sent_main = select(0, MAIN).reshape(owners, MAIN, second)
    sent_last = jnp.pad(select(MAIN, 1), ((0, 0), (0, MAIN * fold - second)))
    sent_last = sent_last.reshape(owners, MAIN, fold)
    sent = jnp.concatenate([sent_main, sent_last], axis=2)
    arrived = lax.all_to_all(sent, "dp", split_axis=0, concat_axis=0, tiled=True)
    arrived_main = arrived[:, :, :second].reshape(owners * MAIN, second)
    arrived_last = arrived[:, :, second:].reshape(owners, MAIN * fold)[:, :second]
    gathered = lax.all_gather(
        jnp.concatenate([arrived_main, arrived_last], axis=0), "expert", axis=0
    )

    first_sent = first_dispatch(row_rank, raw, columns, tok_rows)
    first_rows = lax.all_to_all(first_sent, "dp", split_axis=0, concat_axis=0, tiled=True)

    half = -(-hidden_part // 128) * 128
    pad = ((0, 0), (0, half - hidden_part))
    both = jnp.concatenate([jnp.pad(gate_weight[0], pad), jnp.pad(up_weight[0], pad)], axis=1)
    first_val = jnp.dot(
        first_rows.reshape(slot_rows, first), both[:first], preferred_element_type=f32
    ).reshape(owners, block_rows, 2 * half)
    first_main = first_val[:, : columns * MAIN].reshape(main_rows, 2 * half)
    first_last = jnp.transpose(first_val[:, columns * MAIN :], (1, 0, 2))
    first_val = jnp.concatenate([first_main, first_last.reshape(-1, 2 * half)], axis=0)

    hidden = hidden_rows(gathered, both[first:], first_val, hidden_part)
    full = lax.all_gather(hidden, "expert", axis=0, tiled=True)
    out = lax.dot_general(
        full, down_weight[0], (((0,), (0,)), ((), ())), preferred_element_type=f32
    ).astype(bf16)
    out_main = out[:main_rows].reshape(owners, columns * MAIN, out_width)
    out_last = jnp.transpose(out[main_rows:].reshape(columns, owners, out_width), (1, 0, 2))
    out = jnp.concatenate([out_main, out_last], axis=1)
    back = lax.all_to_all(out, "dp", split_axis=0, concat_axis=0, tiled=True)
    back = back.reshape(slot_rows, out_width)

    raised = jnp.where(picks, jnp.exp(jnp.where(picks, logits, 0.0)), 0.0)
    weights = raised / jnp.sum(raised, axis=1, keepdims=True)
    row_weight = whole_row(weights[:, :owners])
    row = jnp.arange(block_rows, dtype=jnp.int32)
    is_main = row < columns * MAIN
    row_column = jnp.where(is_main, row // MAIN, row - columns * MAIN)
    row_slot = jnp.where(is_main, row % MAIN, MAIN).astype(f32)
    tok_column = jnp.arange(row_toks, dtype=jnp.int32) // tok_rows
    same_column = row_column[:, None] == tok_column[None, :]
    taken = (row_rank == row_slot[None, :, None]) & same_column[None]
    mat = jnp.where(taken, row_weight, 0.0).reshape(slot_rows, row_toks)
    high = lax.reduce_precision(mat, 8, 7)
    low = (mat - high).astype(bf16)
    dims = (((0,), (0,)), ((), ()))
    part = lax.dot_general(high.astype(bf16), back, dims, preferred_element_type=f32)
    part = part + lax.dot_general(low, back, dims, preferred_element_type=f32)
    part = part.astype(bf16).reshape(columns, tok_rows, out_width)
    whole = lax.all_to_all(part, "expert", split_axis=0, concat_axis=0, tiled=True)
    return jnp.transpose(whole, (1, 0, 2)).reshape(tok_rows, model_width)


def solution(mesh):
    in_specs = (
        P(("dp", "expert"), None),
        P(),
        P(("dp", "expert"), None),
        P(("dp", "expert")),
        P("dp", None, "expert"),
        P("dp", None, "expert"),
        P("dp", None, "expert"),
    )
    out_specs = P(("dp", "expert"), None)
    return jax.shard_map(
        per_device, mesh=mesh, in_specs=in_specs, out_specs=out_specs, check_vma=False
    )
```

```python
import functools

import jax
import jax.numpy as jnp
from jax import lax
from jax.experimental import pallas as pl
from jax.experimental.pallas import tpu as pltpu
from jax.sharding import PartitionSpec as P

MAIN = 8
FIRST_WIDTH = 1408
HIDDEN_STEPS = 3
CUT = 4
DISPATCH_STEPS = 1
VMEM_BYTES = 48 * 1024 * 1024
bf16, f32 = jnp.bfloat16, jnp.float32


def iota(shape, dim):
    return lax.broadcasted_iota(jnp.int32, shape, dim)


def first_dispatch_kernel(columns, tok_rows, rank_ref, raw_ref, out_ref, pair_sel, last_sel):
    owners = rank_ref.shape[0]
    pairs = columns // 2
    pair_toks, pair_rows = 2 * tok_rows, 2 * MAIN

    @pl.when(pl.program_id(0) == 0)
    def _():
        row, tok = iota((pair_rows, pair_toks), 0), iota((pair_rows, pair_toks), 1)
        wanted = jnp.where(row // MAIN == tok // tok_rows, row % MAIN, -2).astype(f32)
        for pair in range(pairs):
            rank = rank_ref[:, :, pair * pair_toks : (pair + 1) * pair_toks]
            sel = jnp.where(rank == wanted[None], 1.0, 0.0).astype(bf16)
            pair_sel[pair] = sel.reshape(owners * pair_rows, pair_toks)
        row, tok = iota((columns, columns * tok_rows), 0), iota((columns, columns * tok_rows), 1)
        wanted = jnp.where(row == tok // tok_rows, MAIN, -2).astype(f32)
        sel = jnp.where(rank_ref[...] == wanted[None], 1.0, 0.0)
        last_sel[...] = sel.reshape(owners * columns, columns * tok_rows).astype(bf16)

    for pair in range(pairs):
        rows = jnp.dot(
            pair_sel[pair],
            raw_ref[pair * pair_toks : (pair + 1) * pair_toks, :],
            preferred_element_type=f32,
        ).astype(bf16)
        out_ref[:, pair * pair_rows : (pair + 1) * pair_rows, :] = rows.reshape(
            owners, pair_rows, rows.shape[1]
        )
    rows = jnp.dot(last_sel[...], raw_ref[...], preferred_element_type=f32)
    out_ref[:, columns * MAIN :, :] = rows.reshape(owners, columns, rows.shape[1]).astype(bf16)


def first_dispatch(rank, raw, columns, tok_rows):
    owners = rank.shape[0]
    row_toks, width = raw.shape
    block_rows = columns * (MAIN + 1)
    pairs = columns // 2
    return pl.pallas_call(
        functools.partial(first_dispatch_kernel, columns, tok_rows),
        grid=(DISPATCH_STEPS,),
        in_specs=[
            pl.BlockSpec((owners, 1, row_toks), lambda f: (0, 0, 0)),
            pl.BlockSpec((row_toks, width // DISPATCH_STEPS), lambda f: (0, f)),
        ],
        out_specs=pl.BlockSpec((owners, block_rows, width // DISPATCH_STEPS), lambda f: (0, 0, f)),
        out_shape=jax.ShapeDtypeStruct((owners, block_rows, width), bf16),
        scratch_shapes=[
            pltpu.VMEM((pairs, owners * 2 * MAIN, 2 * tok_rows), bf16),
            pltpu.VMEM((owners * columns, row_toks), bf16),
        ],
        compiler_params=pltpu.CompilerParams(vmem_limit_bytes=VMEM_BYTES),
    )(rank, raw)


def hidden_kernel(rows, cut, x_ref, w_ref, v_ref, near_ref, far_ref, last_sum):
    columns, step_rows, width = x_ref.shape
    half = w_ref.shape[1] // 2
    sources = rows // MAIN
    hidden_part = near_ref.shape[0]
    acc = jnp.dot(
        x_ref[...].reshape(columns * step_rows, width), w_ref[...], preferred_element_type=f32
    )

    def store(ref, val, at):
        gate, up = val[:, :half], val[:, half:]
        hidden = gate / (1.0 + jnp.exp(-gate)) * up
        ref[:, at : at + val.shape[0]] = hidden.T[:hidden_part].astype(bf16)

    def finish(step, blocks, with_last):
        first_source = step * (step_rows // rows) * sources
        for ref, lowest, highest in ((near_ref, 0, cut), (far_ref, cut, columns)):
            count = (highest - lowest) * MAIN
            pieces = [
                acc[(j * step_rows + i) : (j * step_rows + i + MAIN)]
                for i in range(0, blocks * rows, MAIN)
                for j in range(lowest, highest)
            ]
            val = v_ref[first_source : first_source + blocks * sources, lowest * MAIN : highest * MAIN]
            val = val.reshape(blocks * sources * count, 2 * half) + jnp.concatenate(pieces, axis=0)
            store(ref, val, first_source * count)
        if with_last:
            for j in range(columns):
                at = j * step_rows + blocks * rows
                last_sum[j] = acc[at : at + rows]
            val = jnp.concatenate([last_sum[:, i, :] for i in range(rows)], axis=0)
            val = val + v_ref[:, columns * MAIN :].reshape(rows * columns, 2 * half)
            store(far_ref, val, rows * (columns - cut) * MAIN)

    for step in range(HIDDEN_STEPS):
        blocks = step_rows // rows
        with_last = step == HIDDEN_STEPS - 1
        pl.when(pl.program_id(0) == step)(
            functools.partial(finish, step, blocks - with_last, with_last)
        )


def hidden_rows(gathered, weight, first_val, hidden_part, cut):
    columns, col_rows, width = gathered.shape
    owners, block_rows, units = first_val.shape
    steps = HIDDEN_STEPS
    step_rows = col_rows // steps
    near = owners * cut * MAIN
    far = owners * block_rows - near
    return pl.pallas_call(
        functools.partial(hidden_kernel, owners, cut),
        grid=(steps,),
        in_specs=[
            pl.BlockSpec((columns, step_rows, width), lambda b: (0, b, 0)),
            pl.BlockSpec(weight.shape, lambda b: (0, 0)),
            pl.BlockSpec(first_val.shape, lambda b: (0, 0, 0)),
        ],
        out_specs=[
            pl.BlockSpec((hidden_part, near), lambda b: (0, 0)),
            pl.BlockSpec((hidden_part, far), lambda b: (0, 0)),
        ],
        out_shape=[
            jax.ShapeDtypeStruct((hidden_part, near), bf16),
            jax.ShapeDtypeStruct((hidden_part, far), bf16),
        ],
        scratch_shapes=[pltpu.VMEM((columns, owners, units), f32)],
        compiler_params=pltpu.CompilerParams(vmem_limit_bytes=VMEM_BYTES),
    )(gathered, weight, first_val)


def combine_kernel(columns, pair_high, pair_low, last_high, last_low, back_ref, out_ref):
    owners, block_rows, width = back_ref.shape
    pairs, pair_toks, pair_rows = pair_high.shape
    rows = pair_rows // owners
    last = back_ref[:, columns * MAIN :, :].reshape(owners * columns, width)
    for pair in range(pairs):
        back = back_ref[:, pair * rows : (pair + 1) * rows, :].reshape(pair_rows, width)
        toks = slice(pair * pair_toks, (pair + 1) * pair_toks)
        part = jnp.dot(pair_high[pair], back, preferred_element_type=f32)
        part = part + jnp.dot(pair_low[pair], back, preferred_element_type=f32)
        part = part + jnp.dot(last_high[toks], last, preferred_element_type=f32)
        part = part + jnp.dot(last_low[toks], last, preferred_element_type=f32)
        out_ref[toks] = part.astype(bf16)


def combine(mats, back, columns):
    row_toks = mats[2].shape[0]
    return pl.pallas_call(
        functools.partial(combine_kernel, columns),
        out_shape=jax.ShapeDtypeStruct((row_toks, back.shape[2]), bf16),
        compiler_params=pltpu.CompilerParams(vmem_limit_bytes=VMEM_BYTES),
    )(*mats, back)


def combine_matrices(rank, weight, columns, tok_rows):
    row_toks, owners = rank.shape
    high = lax.reduce_precision(weight, 8, 7)
    parts = [high.astype(bf16), (weight - high).astype(bf16)]
    column = jnp.arange(row_toks, dtype=jnp.int32)[:, None] // tok_rows

    def matrix(count, row_column, row_slot):
        lane = jnp.arange(owners * count, dtype=jnp.int32)
        spread = (lane[None, :] // count == jnp.arange(owners, dtype=jnp.int32)[:, None]).astype(bf16)
        wanted = jnp.where(row_column(column, lane % count), row_slot(lane % count), -2).astype(f32)
        mine = jnp.dot(rank, spread, preferred_element_type=f32) == wanted
        return [
            jnp.where(mine, jnp.dot(p, spread, preferred_element_type=f32), 0.0).astype(bf16) for p in parts
        ]

    pairs = columns // 2
    pair = matrix(2 * MAIN, lambda c, r: c % 2 == r[None] // MAIN, lambda r: r[None] % MAIN)
    last = matrix(columns, lambda c, r: c == r[None], lambda r: MAIN)
    return [m.reshape(pairs, 2 * tok_rows, owners * 2 * MAIN) for m in pair] + last


def ordered(blocks):
    columns = len(blocks)
    me = lax.axis_index("expert")
    out = jnp.zeros((columns,) + blocks[0].shape, blocks[0].dtype)
    for distance, block in enumerate(blocks):
        at = ((me + distance) % columns,) + (0,) * block.ndim
        out = lax.dynamic_update_slice(out, block[None], at)
    return out


def gather_small(block):
    columns = lax.axis_size("expert")
    perms = [[((at + d) % columns, at) for at in range(columns)] for d in range(1, columns)]
    return ordered([block] + [lax.ppermute(block, "expert", perm) for perm in perms])


def gather_ring(block):
    columns = lax.axis_size("expert")
    rise = [(at, (at + 1) % columns) for at in range(columns)]
    fall = [(at, (at - 1) % columns) for at in range(columns)]
    below, above = block, block
    blocks = {0: block}
    for distance in range(1, columns // 2):
        below = lax.ppermute(below, "expert", rise)
        above = lax.ppermute(above, "expert", fall)
        blocks[columns - distance] = below
        blocks[distance] = above
    middle = block.shape[0] // 2
    below = lax.ppermute(below[:middle], "expert", rise)
    above = lax.ppermute(above[middle:], "expert", fall)
    blocks[columns // 2] = jnp.concatenate([below, above], axis=0)
    return ordered([blocks[at] for at in range(columns)])


def per_device(tokens, router_weight, rollout_ids, source_row, gate_weight, up_weight, down_weight):
    owners = lax.axis_size("dp")
    columns = lax.axis_size("expert")
    tok_rows, model_width = tokens.shape
    top_count = rollout_ids.shape[1]
    hidden_part = gate_weight.shape[2]
    out_width = down_weight.shape[2]
    block_rows = columns * (MAIN + 1)
    slot_rows = owners * block_rows
    row_toks = columns * tok_rows
    first = FIRST_WIDTH
    second = model_width - first
    fold = -(-second // (MAIN * 128)) * 128

    raw = lax.all_gather(tokens[:, :first], "expert", axis=0, tiled=True)

    logits = jnp.dot(tokens.astype(f32), router_weight, precision=lax.Precision.HIGHEST)

    sent_ids = jnp.broadcast_to(rollout_ids.T[None], (owners, top_count, tok_rows))
    blocks = lax.all_to_all(sent_ids, "dp", split_axis=0, concat_axis=0, tiled=True)
    source_block = source_row[0] // (tok_rows * columns)
    block = lax.dynamic_index_in_dim(blocks, source_block, axis=0, keepdims=False)
    place = (source_row % tok_rows)[None, :] == jnp.arange(tok_rows, dtype=jnp.int32)[:, None]
    expert_ids = jnp.dot(
        block.astype(bf16), place.astype(bf16), preferred_element_type=f32
    ).astype(jnp.int32).T

    expert_iota = jnp.arange(router_weight.shape[1], dtype=jnp.int32)
    picks = jnp.any(expert_ids[:, :, None] == expert_iota[None, None, :], axis=1)
    chosen = picks[:, :owners]
    before = jnp.arange(tok_rows)[:, None] > jnp.arange(tok_rows)[None, :]
    slot_rank = jnp.dot(before.astype(bf16), chosen.astype(bf16), preferred_element_type=f32)
    slot_rank = jnp.where(chosen, slot_rank, -1.0)

    raised = jnp.where(picks, jnp.exp(jnp.where(picks, logits, 0.0)), 0.0)
    weights = raised / jnp.sum(raised, axis=1, keepdims=True)
    def select(lowest, count):
        slots = jnp.arange(lowest, lowest + count, dtype=f32)
        sel = slot_rank[:, :, None] == slots
        sel = sel.reshape(tok_rows, owners * count).astype(bf16)
        return lax.dot_general(
            sel, tokens[:, first:], (((0,), (0,)), ((), ())), preferred_element_type=f32
        ).astype(bf16)

    sent_main = select(0, MAIN).reshape(owners, MAIN, second)
    sent_last = jnp.pad(select(MAIN, 1), ((0, 0), (0, MAIN * fold - second)))
    sent_last = sent_last.reshape(owners, MAIN, fold)
    sent = jnp.concatenate([sent_main, sent_last], axis=2)
    arrived = lax.all_to_all(sent, "dp", split_axis=0, concat_axis=0, tiled=True)
    arrived, rank = lax.optimization_barrier((arrived, slot_rank.T.astype(bf16)))
    rank = lax.all_to_all(
        jnp.broadcast_to(rank[None], (columns,) + rank.shape), "expert", 0, 0, tiled=True
    )
    row_rank = jnp.transpose(rank, (1, 0, 2)).astype(f32).reshape(owners, 1, row_toks)
    tok_rank = jnp.transpose(rank, (0, 2, 1)).reshape(row_toks, owners)
    arrived_main = arrived[:, :, :second].reshape(owners * MAIN, second)
    arrived_last = arrived[:, :, second:].reshape(owners, MAIN * fold)[:, :second]
    gathered = lax.all_gather(
        jnp.concatenate([arrived_main, arrived_last], axis=0), "expert", axis=0
    )

    first_sent = first_dispatch(row_rank, raw, columns, tok_rows)
    weights, first_sent = lax.optimization_barrier((weights[:, :owners].T, first_sent))
    first_rows = lax.all_to_all(first_sent, "dp", split_axis=0, concat_axis=0, tiled=True)

    half = -(-hidden_part // 128) * 128
    pad = ((0, 0), (0, half - hidden_part))
    both = jnp.concatenate([jnp.pad(gate_weight[0], pad), jnp.pad(up_weight[0], pad)], axis=1)
    first_val = jnp.dot(
        first_rows.reshape(slot_rows, first), both[:first], preferred_element_type=f32
    ).reshape(owners, block_rows, 2 * half)
    tok_weight = jnp.transpose(gather_small(weights), (0, 2, 1)).reshape(row_toks, owners)
    mats = combine_matrices(tok_rank, tok_weight, columns, tok_rows)
    mats, first_val = lax.optimization_barrier((mats, first_val))

    near, far = hidden_rows(gathered, both[first:], first_val, hidden_part, CUT)
    far = lax.all_gather(far, "expert", axis=0, tiled=True)
    near = gather_ring(near).reshape(columns * hidden_part, -1)

    def project(full):
        out = lax.dot_general(full, down_weight[0], (((0,), (0,)), ((), ())), preferred_element_type=f32)
        return out.astype(bf16)

    far_main = owners * (columns - CUT) * MAIN
    near, far = project(near), project(far)
    out = jnp.concatenate(
        [
            near.reshape(owners, -1, out_width),
            far[:far_main].reshape(owners, -1, out_width),
            far[far_main:].reshape(owners, columns, out_width),
        ],
        axis=1,
    )
    back = lax.all_to_all(out, "dp", split_axis=0, concat_axis=0, tiled=True)
    part = combine(mats, back, columns).reshape(columns, tok_rows, out_width)
    whole = lax.all_to_all(part, "expert", split_axis=0, concat_axis=0, tiled=True)
    return jnp.transpose(whole, (1, 0, 2)).reshape(tok_rows, model_width)


def solution(mesh):
    in_specs = (
        P(("dp", "expert"), None),
        P(),
        P(("dp", "expert"), None),
        P(("dp", "expert")),
        P("dp", None, "expert"),
        P("dp", None, "expert"),
        P("dp", None, "expert"),
    )
    out_specs = P(("dp", "expert"), None)
    return jax.shard_map(
        per_device, mesh=mesh, in_specs=in_specs, out_specs=out_specs, check_vma=False
    )
```

```python
import functools

import jax
import jax.numpy as jnp
from jax import lax
from jax.experimental import pallas as pl
from jax.experimental.pallas import tpu as pltpu
from jax.sharding import PartitionSpec as P

MAIN = 8
FIRST_WIDTH = 1536
HIDDEN_STEPS = 3
CUT = 4
DISPATCH_STEPS = 1
VMEM_BYTES = 48 * 1024 * 1024
bf16, f32 = jnp.bfloat16, jnp.float32


def iota(shape, dim):
    return lax.broadcasted_iota(jnp.int32, shape, dim)


def first_dispatch_kernel(columns, tok_rows, rank_ref, raw_ref, out_ref, pair_sel, last_sel):
    owners = rank_ref.shape[0]
    pairs = columns // 2
    pair_toks, pair_rows = 2 * tok_rows, 2 * MAIN

    @pl.when(pl.program_id(0) == 0)
    def _():
        row, tok = iota((pair_rows, pair_toks), 0), iota((pair_rows, pair_toks), 1)
        wanted = jnp.where(row // MAIN == tok // tok_rows, row % MAIN, -2).astype(f32)
        for pair in range(pairs):
            rank = rank_ref[:, :, pair * pair_toks : (pair + 1) * pair_toks]
            sel = jnp.where(rank == wanted[None], 1.0, 0.0).astype(bf16)
            pair_sel[pair] = sel.reshape(owners * pair_rows, pair_toks)
        row, tok = iota((columns, columns * tok_rows), 0), iota((columns, columns * tok_rows), 1)
        wanted = jnp.where(row == tok // tok_rows, MAIN, -2).astype(f32)
        sel = jnp.where(rank_ref[...] == wanted[None], 1.0, 0.0)
        last_sel[...] = sel.reshape(owners * columns, columns * tok_rows).astype(bf16)

    for pair in range(pairs):
        rows = jnp.dot(
            pair_sel[pair],
            raw_ref[pair * pair_toks : (pair + 1) * pair_toks, :],
            preferred_element_type=f32,
        ).astype(bf16)
        out_ref[:, pair * pair_rows : (pair + 1) * pair_rows, :] = rows.reshape(
            owners, pair_rows, rows.shape[1]
        )
    rows = jnp.dot(last_sel[...], raw_ref[...], preferred_element_type=f32)
    out_ref[:, columns * MAIN :, :] = rows.reshape(owners, columns, rows.shape[1]).astype(bf16)


def first_dispatch(rank, raw, columns, tok_rows):
    owners = rank.shape[0]
    row_toks, width = raw.shape
    block_rows = columns * (MAIN + 1)
    pairs = columns // 2
    return pl.pallas_call(
        functools.partial(first_dispatch_kernel, columns, tok_rows),
        grid=(DISPATCH_STEPS,),
        in_specs=[
            pl.BlockSpec((owners, 1, row_toks), lambda f: (0, 0, 0)),
            pl.BlockSpec((row_toks, width // DISPATCH_STEPS), lambda f: (0, f)),
        ],
        out_specs=pl.BlockSpec((owners, block_rows, width // DISPATCH_STEPS), lambda f: (0, 0, f)),
        out_shape=jax.ShapeDtypeStruct((owners, block_rows, width), bf16),
        scratch_shapes=[
            pltpu.VMEM((pairs, owners * 2 * MAIN, 2 * tok_rows), bf16),
            pltpu.VMEM((owners * columns, row_toks), bf16),
        ],
        compiler_params=pltpu.CompilerParams(vmem_limit_bytes=VMEM_BYTES),
    )(rank, raw)


def hidden_kernel(rows, cut, x_ref, w_ref, v_ref, near_ref, far_ref, last_sum):
    columns, step_rows, width = x_ref.shape
    units = w_ref.shape[1]
    lanes = 128
    sources = rows // MAIN
    hidden_part = near_ref.shape[0]
    acc = jnp.dot(
        x_ref[...].reshape(columns * step_rows, width), w_ref[...], preferred_element_type=f32
    )

    def silu_times(gate, up):
        return gate / (1.0 + jnp.exp(-gate)) * up

    def store(ref, val, at):
        whole = (units // 2) // lanes * lanes
        tail = val[:, 2 * whole :]
        hidden = jnp.concatenate(
            [
                silu_times(val[:, :whole], val[:, whole : 2 * whole]),
                silu_times(tail, pltpu.roll(tail, lanes // 2, 1)),
            ],
            axis=1,
        )
        ref[:, at : at + val.shape[0]] = hidden.T[:hidden_part].astype(bf16)

    def finish(step, blocks, with_last):
        first_source = step * (step_rows // rows) * sources
        for ref, lowest, highest in ((near_ref, 0, cut), (far_ref, cut, columns)):
            count = (highest - lowest) * MAIN
            pieces = [
                acc[(j * step_rows + i) : (j * step_rows + i + MAIN)]
                for i in range(0, blocks * rows, MAIN)
                for j in range(lowest, highest)
            ]
            val = v_ref[first_source : first_source + blocks * sources, lowest * MAIN : highest * MAIN]
            val = val.reshape(blocks * sources * count, units) + jnp.concatenate(pieces, axis=0)
            store(ref, val, first_source * count)
        if with_last:
            for j in range(columns):
                at = j * step_rows + blocks * rows
                last_sum[j] = acc[at : at + rows]
            val = jnp.concatenate([last_sum[:, i, :] for i in range(rows)], axis=0)
            val = val + v_ref[:, columns * MAIN :].reshape(rows * columns, units)
            store(far_ref, val, rows * (columns - cut) * MAIN)

    for step in range(HIDDEN_STEPS):
        blocks = step_rows // rows
        with_last = step == HIDDEN_STEPS - 1
        pl.when(pl.program_id(0) == step)(
            functools.partial(finish, step, blocks - with_last, with_last)
        )


def hidden_rows(gathered, weight, first_val, hidden_part, cut):
    columns, col_rows, width = gathered.shape
    owners, block_rows, units = first_val.shape
    steps = HIDDEN_STEPS
    step_rows = col_rows // steps
    near = owners * cut * MAIN
    far = owners * block_rows - near
    return pl.pallas_call(
        functools.partial(hidden_kernel, owners, cut),
        grid=(steps,),
        in_specs=[
            pl.BlockSpec((columns, step_rows, width), lambda b: (0, b, 0)),
            pl.BlockSpec(weight.shape, lambda b: (0, 0)),
            pl.BlockSpec(first_val.shape, lambda b: (0, 0, 0)),
        ],
        out_specs=[
            pl.BlockSpec((hidden_part, near), lambda b: (0, 0)),
            pl.BlockSpec((hidden_part, far), lambda b: (0, 0)),
        ],
        out_shape=[
            jax.ShapeDtypeStruct((hidden_part, near), bf16),
            jax.ShapeDtypeStruct((hidden_part, far), bf16),
        ],
        scratch_shapes=[pltpu.VMEM((columns, owners, units), f32)],
        compiler_params=pltpu.CompilerParams(vmem_limit_bytes=VMEM_BYTES),
    )(gathered, weight, first_val)


def combine_kernel(columns, pair_high, pair_low, last_high, last_low, back_ref, out_ref):
    owners, block_rows, width = back_ref.shape
    pairs, pair_toks, pair_rows = pair_high.shape
    rows = pair_rows // owners
    last = back_ref[:, columns * MAIN :, :].reshape(owners * columns, width)
    for pair in range(pairs):
        back = back_ref[:, pair * rows : (pair + 1) * rows, :].reshape(pair_rows, width)
        toks = slice(pair * pair_toks, (pair + 1) * pair_toks)
        part = jnp.dot(pair_high[pair], back, preferred_element_type=f32)
        part = part + jnp.dot(pair_low[pair], back, preferred_element_type=f32)
        part = part + jnp.dot(last_high[toks], last, preferred_element_type=f32)
        part = part + jnp.dot(last_low[toks], last, preferred_element_type=f32)
        out_ref[toks] = part.astype(bf16)


def combine(mats, back, columns):
    row_toks = mats[2].shape[0]
    return pl.pallas_call(
        functools.partial(combine_kernel, columns),
        out_shape=jax.ShapeDtypeStruct((row_toks, back.shape[2]), bf16),
        compiler_params=pltpu.CompilerParams(vmem_limit_bytes=VMEM_BYTES),
    )(*mats, back)


def combine_matrices(rank, weight, columns, tok_rows):
    row_toks, owners = rank.shape
    high = lax.reduce_precision(weight, 8, 7)
    parts = [high.astype(bf16), (weight - high).astype(bf16)]
    column = jnp.arange(row_toks, dtype=jnp.int32)[:, None] // tok_rows

    def matrix(count, row_column, row_slot):
        lane = jnp.arange(owners * count, dtype=jnp.int32)
        spread = (lane[None, :] // count == jnp.arange(owners, dtype=jnp.int32)[:, None]).astype(bf16)
        wanted = jnp.where(row_column(column, lane % count), row_slot(lane % count), -2).astype(f32)
        mine = jnp.dot(rank, spread, preferred_element_type=f32) == wanted
        return [
            jnp.where(mine, jnp.dot(p, spread, preferred_element_type=f32), 0.0).astype(bf16) for p in parts
        ]

    pairs = columns // 2
    pair = matrix(2 * MAIN, lambda c, r: c % 2 == r[None] // MAIN, lambda r: r[None] % MAIN)
    last = matrix(columns, lambda c, r: c == r[None], lambda r: MAIN)
    return [m.reshape(pairs, 2 * tok_rows, owners * 2 * MAIN) for m in pair] + last


def ordered(blocks):
    columns = len(blocks)
    me = lax.axis_index("expert")
    out = jnp.zeros((columns,) + blocks[0].shape, blocks[0].dtype)
    for distance, block in enumerate(blocks):
        at = ((me + distance) % columns,) + (0,) * block.ndim
        out = lax.dynamic_update_slice(out, block[None], at)
    return out


def gather_small(block):
    columns = lax.axis_size("expert")
    perms = [[((at + d) % columns, at) for at in range(columns)] for d in range(1, columns)]
    return ordered([block] + [lax.ppermute(block, "expert", perm) for perm in perms])


def gather_doubling(block):
    columns = lax.axis_size("expert")
    me = lax.axis_index("expert")
    have = block[None]
    distance = 1
    while distance < columns:
        other = lax.ppermute(have, "expert", [(at, at ^ distance) for at in range(columns)])
        upper = (me & distance) != 0
        have = jnp.concatenate([jnp.where(upper, other, have), jnp.where(upper, have, other)], axis=0)
        distance *= 2
    return have


def rings(streams):
    columns = lax.axis_size("expert")
    rise = [(at, (at + 1) % columns) for at in range(columns)]
    fall = [(at, (at - 1) % columns) for at in range(columns)]
    below, above = list(streams), list(streams)
    blocks = [{0: stream} for stream in streams]
    for distance in range(1, columns // 2 + 1):
        farthest = distance == columns // 2
        for k in range(len(streams)):
            if not farthest or k % 2 == 0:
                below[k] = lax.ppermute(below[k], "expert", rise)
                blocks[k][columns - distance] = below[k]
            if not farthest or k % 2 == 1:
                above[k] = lax.ppermute(above[k], "expert", fall)
                blocks[k][distance] = above[k]
    return [[stream[at] for at in range(columns)] for stream in blocks]


def per_device(tokens, router_weight, rollout_ids, source_row, gate_weight, up_weight, down_weight):
    owners = lax.axis_size("dp")
    columns = lax.axis_size("expert")
    tok_rows, model_width = tokens.shape
    top_count = rollout_ids.shape[1]
    hidden_part = gate_weight.shape[2]
    out_width = down_weight.shape[2]
    block_rows = columns * (MAIN + 1)
    slot_rows = owners * block_rows
    row_toks = columns * tok_rows
    first = FIRST_WIDTH
    second = model_width - first
    fold = -(-second // (MAIN * 128)) * 128

    raw = lax.all_gather(tokens[:, :first], "expert", axis=0, tiled=True)

    logits = jnp.dot(tokens.astype(f32), router_weight, precision=lax.Precision.HIGHEST)

    sent_ids = jnp.broadcast_to(rollout_ids.T[None], (owners, top_count, tok_rows))
    blocks = lax.all_to_all(sent_ids, "dp", split_axis=0, concat_axis=0, tiled=True)
    source_block = source_row[0] // (tok_rows * columns)
    block = lax.dynamic_index_in_dim(blocks, source_block, axis=0, keepdims=False)
    place = (source_row % tok_rows)[None, :] == jnp.arange(tok_rows, dtype=jnp.int32)[:, None]
    expert_ids = jnp.dot(
        block.astype(bf16), place.astype(bf16), preferred_element_type=f32
    ).astype(jnp.int32).T

    expert_iota = jnp.arange(router_weight.shape[1], dtype=jnp.int32)
    picks = jnp.any(expert_ids[:, :, None] == expert_iota[None, None, :], axis=1)
    chosen = picks[:, :owners]
    before = jnp.arange(tok_rows)[:, None] > jnp.arange(tok_rows)[None, :]
    slot_rank = jnp.dot(before.astype(bf16), chosen.astype(bf16), preferred_element_type=f32)
    slot_rank = jnp.where(chosen, slot_rank, -1.0)

    def select(lowest, count):
        slots = jnp.arange(lowest, lowest + count, dtype=f32)
        sel = slot_rank[:, :, None] == slots
        sel = sel.reshape(tok_rows, owners * count).astype(bf16)
        return lax.dot_general(
            sel, tokens[:, first:], (((0,), (0,)), ((), ())), preferred_element_type=f32
        ).astype(bf16)

    sent_main = select(0, MAIN).reshape(owners, MAIN, second)
    sent_last = jnp.pad(select(MAIN, 1), ((0, 0), (0, MAIN * fold - second)))
    sent_last = sent_last.reshape(owners, MAIN, fold)
    sent = jnp.concatenate([sent_main, sent_last], axis=2)
    arrived = lax.all_to_all(sent, "dp", split_axis=0, concat_axis=0, tiled=True)
    raised = jnp.where(picks, jnp.exp(jnp.where(picks, logits, 0.0)), 0.0)
    weights = raised / jnp.sum(raised, axis=1, keepdims=True)
    rank = gather_doubling(slot_rank.T.astype(bf16))
    arrived, rank, weights = lax.optimization_barrier((arrived, rank, weights))
    row_rank = jnp.transpose(rank, (1, 0, 2)).astype(f32).reshape(owners, 1, row_toks)
    tok_rank = jnp.transpose(rank, (0, 2, 1)).reshape(row_toks, owners)
    arrived_main = arrived[:, :, :second].reshape(owners * MAIN, second)
    arrived_last = arrived[:, :, second:].reshape(owners, MAIN * fold)[:, :second]
    gathered = lax.all_gather(
        jnp.concatenate([arrived_main, arrived_last], axis=0), "expert", axis=0
    )

    first_sent = first_dispatch(row_rank, raw, columns, tok_rows)
    weights, first_sent = lax.optimization_barrier((weights[:, :owners].T, first_sent))
    first_rows = lax.all_to_all(first_sent, "dp", split_axis=0, concat_axis=0, tiled=True)

    assert hidden_part % 128 == 64
    whole = hidden_part // 128 * 128
    both = jnp.concatenate(
        [part[0][:, a:b] for a, b in ((0, whole), (whole, hidden_part)) for part in (gate_weight, up_weight)],
        axis=1,
    )
    first_val = jnp.dot(
        first_rows.reshape(slot_rows, first), both[:first], preferred_element_type=f32
    ).reshape(owners, block_rows, 2 * hidden_part)
    tok_weight = jnp.transpose(gather_small(weights), (0, 2, 1)).reshape(row_toks, owners)
    mats = combine_matrices(tok_rank, tok_weight, columns, tok_rows)
    mats, first_val = lax.optimization_barrier((mats, first_val))

    near, far = hidden_rows(gathered, both[first:], first_val, hidden_part, CUT)
    near, far = [ordered(blocks).reshape(-1, blocks[0].shape[1]) for blocks in rings([near, far])]

    def project(full):
        out = lax.dot_general(full, down_weight[0], (((0,), (0,)), ((), ())), preferred_element_type=f32)
        return out.astype(bf16)

    far_main = owners * (columns - CUT) * MAIN
    near, far = project(near), project(far)
    out = jnp.concatenate(
        [
            near.reshape(owners, -1, out_width),
            far[:far_main].reshape(owners, -1, out_width),
            far[far_main:].reshape(owners, columns, out_width),
        ],
        axis=1,
    )
    back = lax.all_to_all(out, "dp", split_axis=0, concat_axis=0, tiled=True)
    part = combine(mats, back, columns).reshape(columns, tok_rows, out_width)
    whole = lax.all_to_all(part, "expert", split_axis=0, concat_axis=0, tiled=True)
    return jnp.transpose(whole, (1, 0, 2)).reshape(tok_rows, model_width)


def solution(mesh):
    in_specs = (
        P(("dp", "expert"), None),
        P(),
        P(("dp", "expert"), None),
        P(("dp", "expert")),
        P("dp", None, "expert"),
        P("dp", None, "expert"),
        P("dp", None, "expert"),
    )
    out_specs = P(("dp", "expert"), None)
    return jax.shard_map(
        per_device, mesh=mesh, in_specs=in_specs, out_specs=out_specs, check_vma=False
    )
```

```python
import functools

import jax
import jax.numpy as jnp
from jax import lax
from jax.experimental import pallas as pl
from jax.experimental.pallas import tpu as pltpu
from jax.sharding import PartitionSpec as P

MAIN = 8
FIRST_WIDTH = 1536
HIDDEN_STEPS = 3
CUT = 4
DISPATCH_STEPS = 1
VMEM_BYTES = 48 * 1024 * 1024
bf16, f32 = jnp.bfloat16, jnp.float32


def iota(shape, dim):
    return lax.broadcasted_iota(jnp.int32, shape, dim)


def first_dispatch_kernel(columns, tok_rows, rank_ref, raw_ref, out_ref, pair_sel, last_sel):
    owners = rank_ref.shape[0]
    pairs = columns // 2
    pair_toks, pair_rows = 2 * tok_rows, 2 * MAIN

    @pl.when(pl.program_id(0) == 0)
    def _():
        row, tok = iota((pair_rows, pair_toks), 0), iota((pair_rows, pair_toks), 1)
        wanted = jnp.where(row // MAIN == tok // tok_rows, row % MAIN, -2).astype(f32)
        for pair in range(pairs):
            rank = rank_ref[:, :, pair * pair_toks : (pair + 1) * pair_toks]
            sel = jnp.where(rank == wanted[None], 1.0, 0.0).astype(bf16)
            pair_sel[pair] = sel.reshape(owners * pair_rows, pair_toks)
        row, tok = iota((columns, columns * tok_rows), 0), iota((columns, columns * tok_rows), 1)
        wanted = jnp.where(row == tok // tok_rows, MAIN, -2).astype(f32)
        sel = jnp.where(rank_ref[...] == wanted[None], 1.0, 0.0)
        last_sel[...] = sel.reshape(owners * columns, columns * tok_rows).astype(bf16)

    for pair in range(pairs):
        rows = jnp.dot(
            pair_sel[pair],
            raw_ref[pair * pair_toks : (pair + 1) * pair_toks, :],
            preferred_element_type=f32,
        ).astype(bf16)
        out_ref[:, pair * pair_rows : (pair + 1) * pair_rows, :] = rows.reshape(
            owners, pair_rows, rows.shape[1]
        )
    rows = jnp.dot(last_sel[...], raw_ref[...], preferred_element_type=f32)
    out_ref[:, columns * MAIN :, :] = rows.reshape(owners, columns, rows.shape[1]).astype(bf16)


def first_dispatch(rank, raw, columns, tok_rows):
    owners = rank.shape[0]
    row_toks, width = raw.shape
    block_rows = columns * (MAIN + 1)
    pairs = columns // 2
    return pl.pallas_call(
        functools.partial(first_dispatch_kernel, columns, tok_rows),
        grid=(DISPATCH_STEPS,),
        in_specs=[
            pl.BlockSpec((owners, 1, row_toks), lambda f: (0, 0, 0)),
            pl.BlockSpec((row_toks, width // DISPATCH_STEPS), lambda f: (0, f)),
        ],
        out_specs=pl.BlockSpec((owners, block_rows, width // DISPATCH_STEPS), lambda f: (0, 0, f)),
        out_shape=jax.ShapeDtypeStruct((owners, block_rows, width), bf16),
        scratch_shapes=[
            pltpu.VMEM((pairs, owners * 2 * MAIN, 2 * tok_rows), bf16),
            pltpu.VMEM((owners * columns, row_toks), bf16),
        ],
        compiler_params=pltpu.CompilerParams(vmem_limit_bytes=VMEM_BYTES),
    )(rank, raw)


def hidden_kernel(rows, cut, x_ref, w_ref, v_ref, near_ref, far_ref, last_sum):
    columns, step_rows, width = x_ref.shape
    units = w_ref.shape[1]
    lanes = 128
    sources = rows // MAIN
    hidden_part = near_ref.shape[0]
    acc = jnp.dot(
        x_ref[...].reshape(columns * step_rows, width), w_ref[...], preferred_element_type=f32
    )

    def silu_times(gate, up):
        return gate / (1.0 + jnp.exp(-gate)) * up

    def store(ref, val, at):
        whole = (units // 2) // lanes * lanes
        tail = val[:, 2 * whole :]
        hidden = jnp.concatenate(
            [
                silu_times(val[:, :whole], val[:, whole : 2 * whole]),
                silu_times(tail, pltpu.roll(tail, lanes // 2, 1)),
            ],
            axis=1,
        )
        ref[:, at : at + val.shape[0]] = hidden.T[:hidden_part].astype(bf16)

    def finish(step, blocks, with_last):
        first_source = step * (step_rows // rows) * sources
        for ref, lowest, highest in ((near_ref, 0, cut), (far_ref, cut, columns)):
            count = (highest - lowest) * MAIN
            pieces = [
                acc[(j * step_rows + i) : (j * step_rows + i + MAIN)]
                for i in range(0, blocks * rows, MAIN)
                for j in range(lowest, highest)
            ]
            val = v_ref[first_source : first_source + blocks * sources, lowest * MAIN : highest * MAIN]
            val = val.reshape(blocks * sources * count, units) + jnp.concatenate(pieces, axis=0)
            store(ref, val, first_source * count)
        if with_last:
            for j in range(columns):
                at = j * step_rows + blocks * rows
                last_sum[j] = acc[at : at + rows]
            val = jnp.concatenate([last_sum[:, i, :] for i in range(rows)], axis=0)
            val = val + v_ref[:, columns * MAIN :].reshape(rows * columns, units)
            store(far_ref, val, rows * (columns - cut) * MAIN)

    for step in range(HIDDEN_STEPS):
        blocks = step_rows // rows
        with_last = step == HIDDEN_STEPS - 1
        pl.when(pl.program_id(0) == step)(
            functools.partial(finish, step, blocks - with_last, with_last)
        )


def hidden_rows(gathered, weight, first_val, hidden_part, cut):
    columns, col_rows, width = gathered.shape
    owners, block_rows, units = first_val.shape
    steps = HIDDEN_STEPS
    step_rows = col_rows // steps
    near = owners * cut * MAIN
    far = owners * block_rows - near
    return pl.pallas_call(
        functools.partial(hidden_kernel, owners, cut),
        grid=(steps,),
        in_specs=[
            pl.BlockSpec((columns, step_rows, width), lambda b: (0, b, 0)),
            pl.BlockSpec(weight.shape, lambda b: (0, 0)),
            pl.BlockSpec(first_val.shape, lambda b: (0, 0, 0)),
        ],
        out_specs=[
            pl.BlockSpec((hidden_part, near), lambda b: (0, 0)),
            pl.BlockSpec((hidden_part, far), lambda b: (0, 0)),
        ],
        out_shape=[
            jax.ShapeDtypeStruct((hidden_part, near), bf16),
            jax.ShapeDtypeStruct((hidden_part, far), bf16),
        ],
        scratch_shapes=[pltpu.VMEM((columns, owners, units), f32)],
        compiler_params=pltpu.CompilerParams(vmem_limit_bytes=VMEM_BYTES),
    )(gathered, weight, first_val)


def combine_kernel(columns, pair_high, pair_low, last_high, last_low, back_ref, out_ref):
    owners, block_rows, width = back_ref.shape
    pairs, pair_toks, pair_rows = pair_high.shape
    rows = pair_rows // owners
    last = back_ref[:, columns * MAIN :, :].reshape(owners * columns, width)
    for pair in range(pairs):
        back = back_ref[:, pair * rows : (pair + 1) * rows, :].reshape(pair_rows, width)
        toks = slice(pair * pair_toks, (pair + 1) * pair_toks)
        part = jnp.dot(pair_high[pair], back, preferred_element_type=f32)
        part = part + jnp.dot(pair_low[pair], back, preferred_element_type=f32)
        part = part + jnp.dot(last_high[toks], last, preferred_element_type=f32)
        part = part + jnp.dot(last_low[toks], last, preferred_element_type=f32)
        out_ref[toks] = part.astype(bf16)


def combine(mats, back, columns):
    row_toks = mats[2].shape[0]
    return pl.pallas_call(
        functools.partial(combine_kernel, columns),
        out_shape=jax.ShapeDtypeStruct((row_toks, back.shape[2]), bf16),
        compiler_params=pltpu.CompilerParams(vmem_limit_bytes=VMEM_BYTES),
    )(*mats, back)


def combine_matrices(rank, weight, columns, tok_rows):
    row_toks, owners = rank.shape
    high = lax.reduce_precision(weight, 8, 7)
    parts = [high.astype(bf16), (weight - high).astype(bf16)]
    column = jnp.arange(row_toks, dtype=jnp.int32)[:, None] // tok_rows

    def matrix(count, row_column, row_slot):
        lane = jnp.arange(owners * count, dtype=jnp.int32)
        spread = (lane[None, :] // count == jnp.arange(owners, dtype=jnp.int32)[:, None]).astype(bf16)
        wanted = jnp.where(row_column(column, lane % count), row_slot(lane % count), -2).astype(f32)
        mine = jnp.dot(rank, spread, preferred_element_type=f32) == wanted
        return [
            jnp.where(mine, jnp.dot(p, spread, preferred_element_type=f32), 0.0).astype(bf16) for p in parts
        ]

    pairs = columns // 2
    pair = matrix(2 * MAIN, lambda c, r: c % 2 == r[None] // MAIN, lambda r: r[None] % MAIN)
    last = matrix(columns, lambda c, r: c == r[None], lambda r: MAIN)
    return [m.reshape(pairs, 2 * tok_rows, owners * 2 * MAIN) for m in pair] + last


def ordered(blocks):
    columns = len(blocks)
    me = lax.axis_index("expert")
    out = jnp.zeros((columns,) + blocks[0].shape, blocks[0].dtype)
    for distance, block in enumerate(blocks):
        at = ((me + distance) % columns,) + (0,) * block.ndim
        out = lax.dynamic_update_slice(out, block[None], at)
    return out


def gather_doubling(block):
    columns = lax.axis_size("expert")
    me = lax.axis_index("expert")
    have = block[None]
    distance = 1
    while distance < columns:
        other = lax.ppermute(have, "expert", [(at, at ^ distance) for at in range(columns)])
        upper = (me & distance) != 0
        have = jnp.concatenate([jnp.where(upper, other, have), jnp.where(upper, have, other)], axis=0)
        distance *= 2
    return have


def gather_ring(block):
    columns = lax.axis_size("expert")
    rise = [(at, (at + 1) % columns) for at in range(columns)]
    fall = [(at, (at - 1) % columns) for at in range(columns)]
    below, above = block, block
    blocks = {0: block}
    for distance in range(1, columns // 2):
        below = lax.ppermute(below, "expert", rise)
        above = lax.ppermute(above, "expert", fall)
        blocks[columns - distance] = below
        blocks[distance] = above
    middle = block.shape[0] // 2
    below = lax.ppermute(below[:middle], "expert", rise)
    above = lax.ppermute(above[middle:], "expert", fall)
    blocks[columns // 2] = jnp.concatenate([below, above], axis=0)
    return ordered([blocks[at] for at in range(columns)])


def per_device(tokens, router_weight, rollout_ids, source_row, gate_weight, up_weight, down_weight):
    owners = lax.axis_size("dp")
    columns = lax.axis_size("expert")
    tok_rows, model_width = tokens.shape
    top_count = rollout_ids.shape[1]
    hidden_part = gate_weight.shape[2]
    out_width = down_weight.shape[2]
    block_rows = columns * (MAIN + 1)
    slot_rows = owners * block_rows
    row_toks = columns * tok_rows
    first = FIRST_WIDTH
    second = model_width - first
    fold = -(-second // (MAIN * 128)) * 128

    raw = lax.all_gather(tokens[:, :first], "expert", axis=0, tiled=True)

    logits = jnp.dot(tokens.astype(f32), router_weight, precision=lax.Precision.HIGHEST)

    sent_ids = jnp.broadcast_to(rollout_ids.T[None], (owners, top_count, tok_rows))
    blocks = lax.all_to_all(sent_ids, "dp", split_axis=0, concat_axis=0, tiled=True)
    source_block = source_row[0] // (tok_rows * columns)
    block = lax.dynamic_index_in_dim(blocks, source_block, axis=0, keepdims=False)
    place = (source_row % tok_rows)[None, :] == jnp.arange(tok_rows, dtype=jnp.int32)[:, None]
    expert_ids = jnp.dot(
        block.astype(bf16), place.astype(bf16), preferred_element_type=f32
    ).astype(jnp.int32).T

    expert_iota = jnp.arange(router_weight.shape[1], dtype=jnp.int32)
    picks = jnp.any(expert_ids[:, :, None] == expert_iota[None, None, :], axis=1)
    chosen = picks[:, :owners]
    before = jnp.arange(tok_rows)[:, None] > jnp.arange(tok_rows)[None, :]
    slot_rank = jnp.dot(before.astype(bf16), chosen.astype(bf16), preferred_element_type=f32)
    slot_rank = jnp.where(chosen, slot_rank, -1.0)

    def select(lowest, count):
        slots = jnp.arange(lowest, lowest + count, dtype=f32)
        sel = slot_rank[:, :, None] == slots
        sel = sel.reshape(tok_rows, owners * count).astype(bf16)
        return lax.dot_general(
            sel, tokens[:, first:], (((0,), (0,)), ((), ())), preferred_element_type=f32
        ).astype(bf16)

    sent_main = select(0, MAIN).reshape(owners, MAIN, second)
    sent_last = jnp.pad(select(MAIN, 1), ((0, 0), (0, MAIN * fold - second)))
    sent_last = sent_last.reshape(owners, MAIN, fold)
    sent = jnp.concatenate([sent_main, sent_last], axis=2)
    arrived = lax.all_to_all(sent, "dp", split_axis=0, concat_axis=0, tiled=True)
    raised = jnp.where(picks, jnp.exp(jnp.where(picks, logits, 0.0)), 0.0)
    weights = raised / jnp.sum(raised, axis=1, keepdims=True)
    rank = gather_doubling(slot_rank.T.astype(bf16))
    arrived, rank, weights = lax.optimization_barrier((arrived, rank, weights))
    row_rank = jnp.transpose(rank, (1, 0, 2)).astype(f32).reshape(owners, 1, row_toks)
    tok_rank = jnp.transpose(rank, (0, 2, 1)).reshape(row_toks, owners)
    arrived_main = arrived[:, :, :second].reshape(owners * MAIN, second)
    arrived_last = arrived[:, :, second:].reshape(owners, MAIN * fold)[:, :second]
    gathered = lax.all_gather(
        jnp.concatenate([arrived_main, arrived_last], axis=0), "expert", axis=0
    )

    first_sent = first_dispatch(row_rank, raw, columns, tok_rows)
    weights, first_sent = lax.optimization_barrier((weights[:, :owners].T, first_sent))
    first_rows = lax.all_to_all(first_sent, "dp", split_axis=0, concat_axis=0, tiled=True)

    assert hidden_part % 128 == 64
    whole = hidden_part // 128 * 128
    both = jnp.concatenate(
        [part[0][:, a:b] for a, b in ((0, whole), (whole, hidden_part)) for part in (gate_weight, up_weight)],
        axis=1,
    )
    first_val = jnp.dot(
        first_rows.reshape(slot_rows, first), both[:first], preferred_element_type=f32
    ).reshape(owners, block_rows, 2 * hidden_part)
    tok_weight = jnp.transpose(gather_doubling(weights), (0, 2, 1)).reshape(row_toks, owners)
    mats = combine_matrices(tok_rank, tok_weight, columns, tok_rows)
    mats, first_val = lax.optimization_barrier((mats, first_val))

    near, far = hidden_rows(gathered, both[first:], first_val, hidden_part, CUT)
    far = lax.all_gather(far, "expert", axis=0, tiled=True)
    near = gather_ring(near).reshape(columns * hidden_part, -1)

    def project(full):
        out = lax.dot_general(full, down_weight[0], (((0,), (0,)), ((), ())), preferred_element_type=f32)
        return out.astype(bf16)

    far_main = owners * (columns - CUT) * MAIN
    near, far = project(near), project(far)
    out = jnp.concatenate(
        [
            near.reshape(owners, -1, out_width),
            far[:far_main].reshape(owners, -1, out_width),
            far[far_main:].reshape(owners, columns, out_width),
        ],
        axis=1,
    )
    back = lax.all_to_all(out, "dp", split_axis=0, concat_axis=0, tiled=True)
    part = combine(mats, back, columns).reshape(columns, tok_rows, out_width)
    whole = lax.all_to_all(part, "expert", split_axis=0, concat_axis=0, tiled=True)
    return jnp.transpose(whole, (1, 0, 2)).reshape(tok_rows, model_width)


def solution(mesh):
    in_specs = (
        P(("dp", "expert"), None),
        P(),
        P(("dp", "expert"), None),
        P(("dp", "expert")),
        P("dp", None, "expert"),
        P("dp", None, "expert"),
        P("dp", None, "expert"),
    )
    out_specs = P(("dp", "expert"), None)
    return jax.shard_map(
        per_device, mesh=mesh, in_specs=in_specs, out_specs=out_specs, check_vma=False
    )
```

```python
import functools

import jax
import jax.numpy as jnp
from jax import lax
from jax.experimental import pallas as pl
from jax.experimental.pallas import tpu as pltpu
from jax.sharding import PartitionSpec as P

MAIN = 8
FIRST_WIDTH = 1536
HIDDEN_STEPS = 3
CUT = 4
DISPATCH_STEPS = 1
VMEM_BYTES = 48 * 1024 * 1024
bf16, f32 = jnp.bfloat16, jnp.float32


def iota(shape, dim):
    return lax.broadcasted_iota(jnp.int32, shape, dim)


def first_dispatch_kernel(columns, tok_rows, rank_ref, raw_ref, out_ref, pair_sel, last_sel):
    owners = rank_ref.shape[0]
    pairs = columns // 2
    pair_toks, pair_rows = 2 * tok_rows, 2 * MAIN

    @pl.when(pl.program_id(0) == 0)
    def _():
        row, tok = iota((pair_rows, pair_toks), 0), iota((pair_rows, pair_toks), 1)
        wanted = jnp.where(row // MAIN == tok // tok_rows, row % MAIN, -2).astype(f32)
        for pair in range(pairs):
            rank = rank_ref[:, :, pair * pair_toks : (pair + 1) * pair_toks]
            sel = jnp.where(rank == wanted[None], 1.0, 0.0).astype(bf16)
            pair_sel[pair] = sel.reshape(owners * pair_rows, pair_toks)
        row, tok = iota((columns, columns * tok_rows), 0), iota((columns, columns * tok_rows), 1)
        wanted = jnp.where(row == tok // tok_rows, MAIN, -2).astype(f32)
        sel = jnp.where(rank_ref[...] == wanted[None], 1.0, 0.0)
        last_sel[...] = sel.reshape(owners * columns, columns * tok_rows).astype(bf16)

    for pair in range(pairs):
        rows = jnp.dot(
            pair_sel[pair],
            raw_ref[pair * pair_toks : (pair + 1) * pair_toks, :],
            preferred_element_type=f32,
        ).astype(bf16)
        out_ref[:, pair * pair_rows : (pair + 1) * pair_rows, :] = rows.reshape(
            owners, pair_rows, rows.shape[1]
        )
    rows = jnp.dot(last_sel[...], raw_ref[...], preferred_element_type=f32)
    out_ref[:, columns * MAIN :, :] = rows.reshape(owners, columns, rows.shape[1]).astype(bf16)


def first_dispatch(rank, raw, columns, tok_rows):
    owners = rank.shape[0]
    row_toks, width = raw.shape
    block_rows = columns * (MAIN + 1)
    pairs = columns // 2
    return pl.pallas_call(
        functools.partial(first_dispatch_kernel, columns, tok_rows),
        grid=(DISPATCH_STEPS,),
        in_specs=[
            pl.BlockSpec((owners, 1, row_toks), lambda f: (0, 0, 0)),
            pl.BlockSpec((row_toks, width // DISPATCH_STEPS), lambda f: (0, f)),
        ],
        out_specs=pl.BlockSpec((owners, block_rows, width // DISPATCH_STEPS), lambda f: (0, 0, f)),
        out_shape=jax.ShapeDtypeStruct((owners, block_rows, width), bf16),
        scratch_shapes=[
            pltpu.VMEM((pairs, owners * 2 * MAIN, 2 * tok_rows), bf16),
            pltpu.VMEM((owners * columns, row_toks), bf16),
        ],
        compiler_params=pltpu.CompilerParams(vmem_limit_bytes=VMEM_BYTES),
    )(rank, raw)


def hidden_kernel(rows, cut, x_ref, w_ref, v_ref, near_ref, far_ref, last_sum):
    columns, step_rows, width = x_ref.shape
    units = w_ref.shape[1]
    lanes = 128
    sources = rows // MAIN
    hidden_part = near_ref.shape[0]
    acc = jnp.dot(
        x_ref[...].reshape(columns * step_rows, width), w_ref[...], preferred_element_type=f32
    )

    def silu_times(gate, up):
        return gate / (1.0 + jnp.exp(-gate)) * up

    def store(ref, val, at):
        whole = (units // 2) // lanes * lanes
        tail = val[:, 2 * whole :]
        hidden = jnp.concatenate(
            [
                silu_times(val[:, :whole], val[:, whole : 2 * whole]),
                silu_times(tail, pltpu.roll(tail, lanes // 2, 1)),
            ],
            axis=1,
        )
        ref[:, at : at + val.shape[0]] = hidden.T[:hidden_part].astype(bf16)

    def finish(step, blocks, with_last):
        first_source = step * (step_rows // rows) * sources
        for ref, lowest, highest in ((near_ref, 0, cut), (far_ref, cut, columns)):
            count = (highest - lowest) * MAIN
            pieces = [
                acc[(j * step_rows + i) : (j * step_rows + i + MAIN)]
                for i in range(0, blocks * rows, MAIN)
                for j in range(lowest, highest)
            ]
            val = v_ref[first_source : first_source + blocks * sources, lowest * MAIN : highest * MAIN]
            val = val.reshape(blocks * sources * count, units) + jnp.concatenate(pieces, axis=0)
            store(ref, val, first_source * count)
        if with_last:
            for j in range(columns):
                at = j * step_rows + blocks * rows
                last_sum[j] = acc[at : at + rows]
            val = jnp.concatenate([last_sum[:, i, :] for i in range(rows)], axis=0)
            val = val + v_ref[:, columns * MAIN :].reshape(rows * columns, units)
            store(far_ref, val, rows * (columns - cut) * MAIN)

    for step in range(HIDDEN_STEPS):
        blocks = step_rows // rows
        with_last = step == HIDDEN_STEPS - 1
        pl.when(pl.program_id(0) == step)(
            functools.partial(finish, step, blocks - with_last, with_last)
        )


def hidden_rows(gathered, weight, first_val, hidden_part, cut):
    columns, col_rows, width = gathered.shape
    owners, block_rows, units = first_val.shape
    steps = HIDDEN_STEPS
    step_rows = col_rows // steps
    near = owners * cut * MAIN
    far = owners * block_rows - near
    return pl.pallas_call(
        functools.partial(hidden_kernel, owners, cut),
        grid=(steps,),
        in_specs=[
            pl.BlockSpec((columns, step_rows, width), lambda b: (0, b, 0)),
            pl.BlockSpec(weight.shape, lambda b: (0, 0)),
            pl.BlockSpec(first_val.shape, lambda b: (0, 0, 0)),
        ],
        out_specs=[
            pl.BlockSpec((hidden_part, near), lambda b: (0, 0)),
            pl.BlockSpec((hidden_part, far), lambda b: (0, 0)),
        ],
        out_shape=[
            jax.ShapeDtypeStruct((hidden_part, near), bf16),
            jax.ShapeDtypeStruct((hidden_part, far), bf16),
        ],
        scratch_shapes=[pltpu.VMEM((columns, owners, units), f32)],
        compiler_params=pltpu.CompilerParams(vmem_limit_bytes=VMEM_BYTES),
    )(gathered, weight, first_val)


def combine_kernel(columns, pair_high, pair_low, last_high, last_low, back_ref, out_ref):
    owners, block_rows, width = back_ref.shape
    pairs, pair_toks, pair_rows = pair_high.shape
    rows = pair_rows // owners
    last = back_ref[:, columns * MAIN :, :].reshape(owners * columns, width)
    for pair in range(pairs):
        back = back_ref[:, pair * rows : (pair + 1) * rows, :].reshape(pair_rows, width)
        toks = slice(pair * pair_toks, (pair + 1) * pair_toks)
        part = jnp.dot(pair_high[pair], back, preferred_element_type=f32)
        part = part + jnp.dot(pair_low[pair], back, preferred_element_type=f32)
        part = part + jnp.dot(last_high[toks], last, preferred_element_type=f32)
        part = part + jnp.dot(last_low[toks], last, preferred_element_type=f32)
        out_ref[toks] = part.astype(bf16)


def combine(mats, back, columns):
    row_toks = mats[2].shape[0]
    return pl.pallas_call(
        functools.partial(combine_kernel, columns),
        out_shape=jax.ShapeDtypeStruct((row_toks, back.shape[2]), bf16),
        compiler_params=pltpu.CompilerParams(vmem_limit_bytes=VMEM_BYTES),
    )(*mats, back)


def combine_matrices(rank, weight, columns, tok_rows):
    row_toks, owners = rank.shape
    high = lax.reduce_precision(weight, 8, 7)
    parts = [high.astype(bf16), (weight - high).astype(bf16)]
    column = jnp.arange(row_toks, dtype=jnp.int32)[:, None] // tok_rows

    def matrix(count, row_column, row_slot):
        lane = jnp.arange(owners * count, dtype=jnp.int32)
        spread = (lane[None, :] // count == jnp.arange(owners, dtype=jnp.int32)[:, None]).astype(bf16)
        wanted = jnp.where(row_column(column, lane % count), row_slot(lane % count), -2).astype(f32)
        mine = jnp.dot(rank, spread, preferred_element_type=f32) == wanted
        return [
            jnp.where(mine, jnp.dot(p, spread, preferred_element_type=f32), 0.0).astype(bf16) for p in parts
        ]

    pairs = columns // 2
    pair = matrix(2 * MAIN, lambda c, r: c % 2 == r[None] // MAIN, lambda r: r[None] % MAIN)
    last = matrix(columns, lambda c, r: c == r[None], lambda r: MAIN)
    return [m.reshape(pairs, 2 * tok_rows, owners * 2 * MAIN) for m in pair] + last


def ordered(blocks):
    columns = len(blocks)
    me = lax.axis_index("expert")
    out = jnp.zeros((columns,) + blocks[0].shape, blocks[0].dtype)
    for distance, block in enumerate(blocks):
        at = ((me + distance) % columns,) + (0,) * block.ndim
        out = lax.dynamic_update_slice(out, block[None], at)
    return out


def gather_doubling(block):
    columns = lax.axis_size("expert")
    me = lax.axis_index("expert")
    have = block[None]
    distance = 1
    while distance < columns:
        other = lax.ppermute(have, "expert", [(at, at ^ distance) for at in range(columns)])
        upper = (me & distance) != 0
        have = jnp.concatenate([jnp.where(upper, other, have), jnp.where(upper, have, other)], axis=0)
        distance *= 2
    return have


def rings(streams):
    columns = lax.axis_size("expert")
    rise = [(at, (at + 1) % columns) for at in range(columns)]
    fall = [(at, (at - 1) % columns) for at in range(columns)]
    below, above = list(streams), list(streams)
    blocks = [{0: stream} for stream in streams]
    for distance in range(1, columns // 2 + 1):
        farthest = distance == columns // 2
        for k in range(len(streams)):
            if not farthest or k % 2 == 0:
                below[k] = lax.ppermute(below[k], "expert", rise)
                blocks[k][columns - distance] = below[k]
            if not farthest or k % 2 == 1:
                above[k] = lax.ppermute(above[k], "expert", fall)
                blocks[k][distance] = above[k]
    return [[stream[at] for at in range(columns)] for stream in blocks]


def per_device(tokens, router_weight, rollout_ids, source_row, gate_weight, up_weight, down_weight):
    owners = lax.axis_size("dp")
    columns = lax.axis_size("expert")
    tok_rows, model_width = tokens.shape
    top_count = rollout_ids.shape[1]
    hidden_part = gate_weight.shape[2]
    out_width = down_weight.shape[2]
    block_rows = columns * (MAIN + 1)
    slot_rows = owners * block_rows
    row_toks = columns * tok_rows
    first = FIRST_WIDTH
    second = model_width - first
    fold = -(-second // (MAIN * 128)) * 128

    raw = lax.all_gather(tokens[:, :first], "expert", axis=0, tiled=True)

    logits = jnp.dot(tokens.astype(f32), router_weight, precision=lax.Precision.HIGHEST)

    sent_ids = jnp.broadcast_to(rollout_ids.T[None], (owners, top_count, tok_rows))
    blocks = lax.all_to_all(sent_ids, "dp", split_axis=0, concat_axis=0, tiled=True)
    source_block = source_row[0] // (tok_rows * columns)
    block = lax.dynamic_index_in_dim(blocks, source_block, axis=0, keepdims=False)
    place = (source_row % tok_rows)[None, :] == jnp.arange(tok_rows, dtype=jnp.int32)[:, None]
    expert_ids = jnp.dot(
        block.astype(bf16), place.astype(bf16), preferred_element_type=f32
    ).astype(jnp.int32).T

    expert_iota = jnp.arange(router_weight.shape[1], dtype=jnp.int32)
    picks = jnp.any(expert_ids[:, :, None] == expert_iota[None, None, :], axis=1)
    chosen = picks[:, :owners]
    before = jnp.arange(tok_rows)[:, None] > jnp.arange(tok_rows)[None, :]
    slot_rank = jnp.dot(before.astype(bf16), chosen.astype(bf16), preferred_element_type=f32)
    slot_rank = jnp.where(chosen, slot_rank, -1.0)

    def select(lowest, count):
        slots = jnp.arange(lowest, lowest + count, dtype=f32)
        sel = slot_rank[:, :, None] == slots
        sel = sel.reshape(tok_rows, owners * count).astype(bf16)
        return lax.dot_general(
            sel, tokens[:, first:], (((0,), (0,)), ((), ())), preferred_element_type=f32
        ).astype(bf16)

    sent_main = select(0, MAIN).reshape(owners, MAIN, second)
    sent_last = jnp.pad(select(MAIN, 1), ((0, 0), (0, MAIN * fold - second)))
    sent_last = sent_last.reshape(owners, MAIN, fold)
    sent = jnp.concatenate([sent_main, sent_last], axis=2)
    arrived = lax.all_to_all(sent, "dp", split_axis=0, concat_axis=0, tiled=True)
    raised = jnp.where(picks, jnp.exp(jnp.where(picks, logits, 0.0)), 0.0)
    weights = raised / jnp.sum(raised, axis=1, keepdims=True)
    rank = gather_doubling(slot_rank.T.astype(bf16))
    arrived, rank, weights = lax.optimization_barrier((arrived, rank, weights))
    row_rank = jnp.transpose(rank, (1, 0, 2)).astype(f32).reshape(owners, 1, row_toks)
    tok_rank = jnp.transpose(rank, (0, 2, 1)).reshape(row_toks, owners)
    arrived_main = arrived[:, :, :second].reshape(owners * MAIN, second)
    arrived_last = arrived[:, :, second:].reshape(owners, MAIN * fold)[:, :second]
    gathered = lax.all_gather(
        jnp.concatenate([arrived_main, arrived_last], axis=0), "expert", axis=0
    )

    first_sent = first_dispatch(row_rank, raw, columns, tok_rows)
    weights, first_sent = lax.optimization_barrier((weights[:, :owners].T, first_sent))
    first_rows = lax.all_to_all(first_sent, "dp", split_axis=0, concat_axis=0, tiled=True)

    assert hidden_part % 128 == 64
    whole = hidden_part // 128 * 128
    both = jnp.concatenate(
        [part[0][:, a:b] for a, b in ((0, whole), (whole, hidden_part)) for part in (gate_weight, up_weight)],
        axis=1,
    )
    first_val = jnp.dot(
        first_rows.reshape(slot_rows, first), both[:first], preferred_element_type=f32
    ).reshape(owners, block_rows, 2 * hidden_part)
    tok_weight = jnp.transpose(gather_doubling(weights), (0, 2, 1)).reshape(row_toks, owners)
    mats = combine_matrices(tok_rank, tok_weight, columns, tok_rows)
    mats, first_val = lax.optimization_barrier((mats, first_val))

    near, far = hidden_rows(gathered, both[first:], first_val, hidden_part, CUT)
    near, far = [ordered(blocks).reshape(-1, blocks[0].shape[1]) for blocks in rings([near, far])]

    def project(full):
        out = lax.dot_general(full, down_weight[0], (((0,), (0,)), ((), ())), preferred_element_type=f32)
        return out.astype(bf16)

    far_main = owners * (columns - CUT) * MAIN
    near, far = project(near), project(far)
    out = jnp.concatenate(
        [
            near.reshape(owners, -1, out_width),
            far[:far_main].reshape(owners, -1, out_width),
            far[far_main:].reshape(owners, columns, out_width),
        ],
        axis=1,
    )
    back = lax.all_to_all(out, "dp", split_axis=0, concat_axis=0, tiled=True)
    part = combine(mats, back, columns).reshape(columns, tok_rows, out_width)
    whole = lax.all_to_all(part, "expert", split_axis=0, concat_axis=0, tiled=True)
    return jnp.transpose(whole, (1, 0, 2)).reshape(tok_rows, model_width)


def solution(mesh):
    in_specs = (
        P(("dp", "expert"), None),
        P(),
        P(("dp", "expert"), None),
        P(("dp", "expert")),
        P("dp", None, "expert"),
        P("dp", None, "expert"),
        P("dp", None, "expert"),
    )
    out_specs = P(("dp", "expert"), None)
    return jax.shard_map(
        per_device, mesh=mesh, in_specs=in_specs, out_specs=out_specs, check_vma=False
    )
```

```python
import functools

import jax
import jax.numpy as jnp
from jax import lax
from jax.experimental import pallas as pl
from jax.experimental.pallas import tpu as pltpu
from jax.sharding import PartitionSpec as P

MAIN = 8
FIRST_WIDTH = 1536
HIDDEN_STEPS = 3
CUT = 4
DISPATCH_STEPS = 2
VMEM_BYTES = 48 * 1024 * 1024
bf16, f32 = jnp.bfloat16, jnp.float32


def iota(shape, dim):
    return lax.broadcasted_iota(jnp.int32, shape, dim)


def first_dispatch_kernel(columns, tok_rows, rank_ref, raw_ref, out_ref, pair_sel, last_sel):
    owners = rank_ref.shape[0]
    pairs = columns // 2
    pair_toks, pair_rows = 2 * tok_rows, 2 * MAIN

    @pl.when(pl.program_id(0) == 0)
    def _():
        row, tok = iota((pair_rows, pair_toks), 0), iota((pair_rows, pair_toks), 1)
        wanted = jnp.where(row // MAIN == tok // tok_rows, row % MAIN, -2).astype(f32)
        for pair in range(pairs):
            rank = rank_ref[:, :, pair * pair_toks : (pair + 1) * pair_toks]
            sel = jnp.where(rank == wanted[None], 1.0, 0.0).astype(bf16)
            pair_sel[pair] = sel.reshape(owners * pair_rows, pair_toks)
        row, tok = iota((columns, columns * tok_rows), 0), iota((columns, columns * tok_rows), 1)
        wanted = jnp.where(row == tok // tok_rows, MAIN, -2).astype(f32)
        sel = jnp.where(rank_ref[...] == wanted[None], 1.0, 0.0)
        last_sel[...] = sel.reshape(owners * columns, columns * tok_rows).astype(bf16)

    for pair in range(pairs):
        rows = jnp.dot(
            pair_sel[pair],
            raw_ref[pair * pair_toks : (pair + 1) * pair_toks, :],
            preferred_element_type=f32,
        ).astype(bf16)
        out_ref[:, pair * pair_rows : (pair + 1) * pair_rows, :] = rows.reshape(
            owners, pair_rows, rows.shape[1]
        )
    rows = jnp.dot(last_sel[...], raw_ref[...], preferred_element_type=f32)
    out_ref[:, columns * MAIN :, :] = rows.reshape(owners, columns, rows.shape[1]).astype(bf16)


def first_dispatch(rank, raw, columns, tok_rows):
    owners = rank.shape[0]
    row_toks, width = raw.shape
    block_rows = columns * (MAIN + 1)
    pairs = columns // 2
    return pl.pallas_call(
        functools.partial(first_dispatch_kernel, columns, tok_rows),
        grid=(DISPATCH_STEPS,),
        in_specs=[
            pl.BlockSpec((owners, 1, row_toks), lambda f: (0, 0, 0)),
            pl.BlockSpec((row_toks, width // DISPATCH_STEPS), lambda f: (0, f)),
        ],
        out_specs=pl.BlockSpec((owners, block_rows, width // DISPATCH_STEPS), lambda f: (0, 0, f)),
        out_shape=jax.ShapeDtypeStruct((owners, block_rows, width), bf16),
        scratch_shapes=[
            pltpu.VMEM((pairs, owners * 2 * MAIN, 2 * tok_rows), bf16),
            pltpu.VMEM((owners * columns, row_toks), bf16),
        ],
        compiler_params=pltpu.CompilerParams(vmem_limit_bytes=VMEM_BYTES),
    )(rank, raw)


def hidden_kernel(rows, cut, x_ref, w_ref, v_ref, near_ref, far_ref, last_sum):
    columns, step_rows, width = x_ref.shape
    units = w_ref.shape[1]
    lanes = 128
    sources = rows // MAIN
    hidden_part = near_ref.shape[0]
    acc = jnp.dot(
        x_ref[...].reshape(columns * step_rows, width), w_ref[...], preferred_element_type=f32
    )

    def silu_times(gate, up):
        return gate / (1.0 + jnp.exp(-gate)) * up

    def store(ref, val, at):
        whole = (units // 2) // lanes * lanes
        tail = val[:, 2 * whole :]
        hidden = jnp.concatenate(
            [
                silu_times(val[:, :whole], val[:, whole : 2 * whole]),
                silu_times(tail, pltpu.roll(tail, lanes // 2, 1)),
            ],
            axis=1,
        )
        ref[:, at : at + val.shape[0]] = hidden.T[:hidden_part].astype(bf16)

    def finish(step, blocks, with_last):
        first_source = step * (step_rows // rows) * sources
        for ref, lowest, highest in ((near_ref, 0, cut), (far_ref, cut, columns)):
            count = (highest - lowest) * MAIN
            pieces = [
                acc[(j * step_rows + i) : (j * step_rows + i + MAIN)]
                for i in range(0, blocks * rows, MAIN)
                for j in range(lowest, highest)
            ]
            val = v_ref[first_source : first_source + blocks * sources, lowest * MAIN : highest * MAIN]
            val = val.reshape(blocks * sources * count, units) + jnp.concatenate(pieces, axis=0)
            store(ref, val, first_source * count)
        if with_last:
            for j in range(columns):
                at = j * step_rows + blocks * rows
                last_sum[j] = acc[at : at + rows]
            val = jnp.concatenate([last_sum[:, i, :] for i in range(rows)], axis=0)
            val = val + v_ref[:, columns * MAIN :].reshape(rows * columns, units)
            store(far_ref, val, rows * (columns - cut) * MAIN)

    for step in range(HIDDEN_STEPS):
        blocks = step_rows // rows
        with_last = step == HIDDEN_STEPS - 1
        pl.when(pl.program_id(0) == step)(
            functools.partial(finish, step, blocks - with_last, with_last)
        )


def hidden_rows(gathered, weight, first_val, hidden_part, cut):
    columns, col_rows, width = gathered.shape
    owners, block_rows, units = first_val.shape
    steps = HIDDEN_STEPS
    step_rows = col_rows // steps
    near = owners * cut * MAIN
    far = owners * block_rows - near
    return pl.pallas_call(
        functools.partial(hidden_kernel, owners, cut),
        grid=(steps,),
        in_specs=[
            pl.BlockSpec((columns, step_rows, width), lambda b: (0, b, 0)),
            pl.BlockSpec(weight.shape, lambda b: (0, 0)),
            pl.BlockSpec(first_val.shape, lambda b: (0, 0, 0)),
        ],
        out_specs=[
            pl.BlockSpec((hidden_part, near), lambda b: (0, 0)),
            pl.BlockSpec((hidden_part, far), lambda b: (0, 0)),
        ],
        out_shape=[
            jax.ShapeDtypeStruct((hidden_part, near), bf16),
            jax.ShapeDtypeStruct((hidden_part, far), bf16),
        ],
        scratch_shapes=[pltpu.VMEM((columns, owners, units), f32)],
        compiler_params=pltpu.CompilerParams(vmem_limit_bytes=VMEM_BYTES),
    )(gathered, weight, first_val)


def combine_kernel(columns, pair_high, pair_low, last_high, last_low, back_ref, out_ref):
    owners, block_rows, width = back_ref.shape
    pairs, pair_toks, pair_rows = pair_high.shape
    rows = pair_rows // owners
    last = back_ref[:, columns * MAIN :, :].reshape(owners * columns, width)
    for pair in range(pairs):
        back = back_ref[:, pair * rows : (pair + 1) * rows, :].reshape(pair_rows, width)
        toks = slice(pair * pair_toks, (pair + 1) * pair_toks)
        part = jnp.dot(pair_high[pair], back, preferred_element_type=f32)
        part = part + jnp.dot(pair_low[pair], back, preferred_element_type=f32)
        part = part + jnp.dot(last_high[toks], last, preferred_element_type=f32)
        part = part + jnp.dot(last_low[toks], last, preferred_element_type=f32)
        out_ref[toks] = part.astype(bf16)


def combine(mats, back, columns):
    row_toks = mats[2].shape[0]
    return pl.pallas_call(
        functools.partial(combine_kernel, columns),
        out_shape=jax.ShapeDtypeStruct((row_toks, back.shape[2]), bf16),
        compiler_params=pltpu.CompilerParams(vmem_limit_bytes=VMEM_BYTES),
    )(*mats, back)


def combine_matrices(rank, weight, columns, tok_rows):
    row_toks, owners = rank.shape
    high = lax.reduce_precision(weight, 8, 7)
    parts = [high.astype(bf16), (weight - high).astype(bf16)]
    column = jnp.arange(row_toks, dtype=jnp.int32)[:, None] // tok_rows

    def matrix(count, row_column, row_slot):
        lane = jnp.arange(owners * count, dtype=jnp.int32)
        spread = (lane[None, :] // count == jnp.arange(owners, dtype=jnp.int32)[:, None]).astype(bf16)
        wanted = jnp.where(row_column(column, lane % count), row_slot(lane % count), -2).astype(f32)
        mine = jnp.dot(rank, spread, preferred_element_type=f32) == wanted
        return [
            jnp.where(mine, jnp.dot(p, spread, preferred_element_type=f32), 0.0).astype(bf16) for p in parts
        ]

    pairs = columns // 2
    pair = matrix(2 * MAIN, lambda c, r: c % 2 == r[None] // MAIN, lambda r: r[None] % MAIN)
    last = matrix(columns, lambda c, r: c == r[None], lambda r: MAIN)
    return [m.reshape(pairs, 2 * tok_rows, owners * 2 * MAIN) for m in pair] + last


def ordered(blocks):
    columns = len(blocks)
    me = lax.axis_index("expert")
    out = jnp.zeros((columns,) + blocks[0].shape, blocks[0].dtype)
    for distance, block in enumerate(blocks):
        at = ((me + distance) % columns,) + (0,) * block.ndim
        out = lax.dynamic_update_slice(out, block[None], at)
    return out


def gather_doubling(block):
    columns = lax.axis_size("expert")
    me = lax.axis_index("expert")
    have = block[None]
    distance = 1
    while distance < columns:
        other = lax.ppermute(have, "expert", [(at, at ^ distance) for at in range(columns)])
        upper = (me & distance) != 0
        have = jnp.concatenate([jnp.where(upper, other, have), jnp.where(upper, have, other)], axis=0)
        distance *= 2
    return have


def gather_ring(block):
    columns = lax.axis_size("expert")
    rise = [(at, (at + 1) % columns) for at in range(columns)]
    fall = [(at, (at - 1) % columns) for at in range(columns)]
    below, above = block, block
    blocks = {0: block}
    for distance in range(1, columns // 2):
        below = lax.ppermute(below, "expert", rise)
        above = lax.ppermute(above, "expert", fall)
        blocks[columns - distance] = below
        blocks[distance] = above
    middle = block.shape[0] // 2
    below = lax.ppermute(below[:middle], "expert", rise)
    above = lax.ppermute(above[middle:], "expert", fall)
    blocks[columns // 2] = jnp.concatenate([below, above], axis=0)
    return ordered([blocks[at] for at in range(columns)])


def per_device(tokens, router_weight, rollout_ids, source_row, gate_weight, up_weight, down_weight):
    owners = lax.axis_size("dp")
    columns = lax.axis_size("expert")
    tok_rows, model_width = tokens.shape
    top_count = rollout_ids.shape[1]
    hidden_part = gate_weight.shape[2]
    out_width = down_weight.shape[2]
    block_rows = columns * (MAIN + 1)
    slot_rows = owners * block_rows
    row_toks = columns * tok_rows
    first = FIRST_WIDTH
    second = model_width - first
    fold = -(-second // (MAIN * 128)) * 128

    raw = lax.all_gather(tokens[:, :first], "expert", axis=0, tiled=True)

    logits = jnp.dot(tokens.astype(f32), router_weight, precision=lax.Precision.HIGHEST)

    sent_ids = jnp.broadcast_to(rollout_ids.T[None], (owners, top_count, tok_rows))
    blocks = lax.all_to_all(sent_ids, "dp", split_axis=0, concat_axis=0, tiled=True)
    source_block = source_row[0] // (tok_rows * columns)
    block = lax.dynamic_index_in_dim(blocks, source_block, axis=0, keepdims=False)
    place = (source_row % tok_rows)[None, :] == jnp.arange(tok_rows, dtype=jnp.int32)[:, None]
    expert_ids = jnp.dot(
        block.astype(bf16), place.astype(bf16), preferred_element_type=f32
    ).astype(jnp.int32).T

    expert_iota = jnp.arange(router_weight.shape[1], dtype=jnp.int32)
    picks = jnp.any(expert_ids[:, :, None] == expert_iota[None, None, :], axis=1)
    chosen = picks[:, :owners]
    before = jnp.arange(tok_rows)[:, None] > jnp.arange(tok_rows)[None, :]
    slot_rank = jnp.dot(before.astype(bf16), chosen.astype(bf16), preferred_element_type=f32)
    slot_rank = jnp.where(chosen, slot_rank, -1.0)

    def select(lowest, count):
        slots = jnp.arange(lowest, lowest + count, dtype=f32)
        sel = slot_rank[:, :, None] == slots
        sel = sel.reshape(tok_rows, owners * count).astype(bf16)
        return lax.dot_general(
            sel, tokens[:, first:], (((0,), (0,)), ((), ())), preferred_element_type=f32
        ).astype(bf16)

    sent_main = select(0, MAIN).reshape(owners, MAIN, second)
    sent_last = jnp.pad(select(MAIN, 1), ((0, 0), (0, MAIN * fold - second)))
    sent_last = sent_last.reshape(owners, MAIN, fold)
    sent = jnp.concatenate([sent_main, sent_last], axis=2)
    arrived = lax.all_to_all(sent, "dp", split_axis=0, concat_axis=0, tiled=True)
    raised = jnp.where(picks, jnp.exp(jnp.where(picks, logits, 0.0)), 0.0)
    weights = raised / jnp.sum(raised, axis=1, keepdims=True)
    rank = gather_doubling(slot_rank.T.astype(bf16))
    arrived, rank, weights = lax.optimization_barrier((arrived, rank, weights))
    row_rank = jnp.transpose(rank, (1, 0, 2)).astype(f32).reshape(owners, 1, row_toks)
    tok_rank = jnp.transpose(rank, (0, 2, 1)).reshape(row_toks, owners)
    arrived_main = arrived[:, :, :second].reshape(owners * MAIN, second)
    arrived_last = arrived[:, :, second:].reshape(owners, MAIN * fold)[:, :second]
    gathered = lax.all_gather(
        jnp.concatenate([arrived_main, arrived_last], axis=0), "expert", axis=0
    )

    first_sent = first_dispatch(row_rank, raw, columns, tok_rows)
    weights, first_sent = lax.optimization_barrier((weights[:, :owners].T, first_sent))
    first_rows = lax.all_to_all(first_sent, "dp", split_axis=0, concat_axis=0, tiled=True)

    assert hidden_part % 128 == 64
    whole = hidden_part // 128 * 128
    both = jnp.concatenate(
        [part[0][:, a:b] for a, b in ((0, whole), (whole, hidden_part)) for part in (gate_weight, up_weight)],
        axis=1,
    )
    first_val = jnp.dot(
        first_rows.reshape(slot_rows, first), both[:first], preferred_element_type=f32
    ).reshape(owners, block_rows, 2 * hidden_part)
    tok_weight = jnp.transpose(gather_doubling(weights), (0, 2, 1)).reshape(row_toks, owners)
    mats = combine_matrices(tok_rank, tok_weight, columns, tok_rows)
    mats, first_val = lax.optimization_barrier((mats, first_val))

    near, far = hidden_rows(gathered, both[first:], first_val, hidden_part, CUT)
    far = lax.all_gather(far, "expert", axis=0, tiled=True)
    near = gather_ring(near).reshape(columns * hidden_part, -1)

    def project(full):
        out = lax.dot_general(full, down_weight[0], (((0,), (0,)), ((), ())), preferred_element_type=f32)
        return out.astype(bf16)

    far_main = owners * (columns - CUT) * MAIN
    near, far = project(near), project(far)
    out = jnp.concatenate(
        [
            near.reshape(owners, -1, out_width),
            far[:far_main].reshape(owners, -1, out_width),
            far[far_main:].reshape(owners, columns, out_width),
        ],
        axis=1,
    )
    back = lax.all_to_all(out, "dp", split_axis=0, concat_axis=0, tiled=True)
    part = combine(mats, back, columns).reshape(columns, tok_rows, out_width)
    whole = lax.all_to_all(part, "expert", split_axis=0, concat_axis=0, tiled=True)
    return jnp.transpose(whole, (1, 0, 2)).reshape(tok_rows, model_width)


def solution(mesh):
    in_specs = (
        P(("dp", "expert"), None),
        P(),
        P(("dp", "expert"), None),
        P(("dp", "expert")),
        P("dp", None, "expert"),
        P("dp", None, "expert"),
        P("dp", None, "expert"),
    )
    out_specs = P(("dp", "expert"), None)
    return jax.shard_map(
        per_device, mesh=mesh, in_specs=in_specs, out_specs=out_specs, check_vma=False
    )
```
